512 devices in a mesh: dp: 32 (over x, z_lo, core), ctx: 16 (over z_hi, y).
Axes of the slice: x: 4, y: 4, z: 16 (z_hi: 4, z_lo: 4; z = z_hi * 4 + z_lo), core: 2. Of those that a mesh axis runs over, the one named last changes fastest.
Arguments:
- grad_out: bfloat16 [16384, 8192], P('ctx', 'dp'), may hold values from -6 to 6
- conv_input: bfloat16 [16384, 8192], P('ctx', 'dp'), may hold values from -6 to 6
- residues: float32 [256, 8], replicated, may hold values from -0.12 to 0.12
- log_rate: float32 [256, 8], replicated, as said below
Outputs:
- grad_input: bfloat16 [16384, 8192], P('ctx', 'dp')
- grad_residue: float32 [256, 8], P('ctx')
- grad_lograte: float32 [256, 8], P('ctx')
The draws below stay inside these ranges and needn't reach their ends.
Inputs may be any that keep to these rules, and one draw needn't show every extreme that they name: The rates exp(log_rate) lie between 0.1 / 16384 and 1 / 16.
All inputs are finite; a program needn't handle non-finite values.
Results may differ from the reference program's by a relative error of at most 0.014.
Values may be sent and summed in bfloat16 or wider, within the bound.
No kernel may reach another device: no remote copies, remote signals or barrier semaphores. Data moves between devices by JAX's collectives and lax.ppermute only.
A program may use at most 64 MiB of HBM per device.

```python
import math
import jax
import jax.numpy as jnp
from jax import lax

C = 8192
FG = 256
M = 8
SEQ = 16384


def draw_log_rate(key, part):
    key = jax.random.fold_in(key, 7)
    first, second, third = jax.random.split(key, 3)
    share = 0.5
    slow_lo = math.log(0.1 / SEQ)
    slow_hi = math.log(2.0 / SEQ)
    fast_hi = math.log(1.0 / 16.0)
    slow = jax.random.uniform(first, (FG, M), jnp.float32) < share
    slow_val = slow_lo + (slow_hi - slow_lo) * jax.random.uniform(second, (FG, M), jnp.float32)
    fast_val = slow_hi + (fast_hi - slow_hi) * jax.random.uniform(third, (FG, M), jnp.float32)
    return jnp.where(slow, slow_val, fast_val).astype(jnp.float32)


def spiked(result, stream_key, source, target, parts, factor):
    def block_of(position):
        return (jnp.arange(result.shape[position]) // (result.shape[position] // parts)).reshape((-1,) + (1,) * (result.ndim - 1 - position))

    first = jax.random.permutation(stream_key, parts)[block_of(target)]
    second = (block_of(target) + parts // 2) % parts
    return jnp.where((block_of(source) == first) | (block_of(source) == second), factor * result, result)


def block_scale(key, shape, shards, smallest, top_value):
    level, own = 1.0, jax.random.fold_in(key, 6)
    for dim, parts in shards:
        draws = jnp.exp(jax.random.uniform(jax.random.fold_in(own, dim), (parts,), jnp.float32, smallest / len(shards), top_value / len(shards)))
        level = level * jnp.repeat(draws, shape[dim] // parts).reshape([-1 if axis == dim else 1 for axis in range(len(shape))])
    return level


def scatter_about(rng, dims, scale, limit, cuts=(), kind=jnp.bfloat16):
    values = jax.random.normal(rng, dims, jnp.float32) * scale
    if len(cuts) > 0:
        values = block_scale(rng, dims, cuts, -0.22, 0.18) * values
    return jnp.clip(values, min=-limit, max=limit).astype(kind)


def bell_draw_with(rng, extent, scale, reach, cuts, heavy, held_as=jnp.bfloat16):
    drawn = scale * jax.random.normal(rng, extent, jnp.float32)
    if cuts:
        drawn = drawn * block_scale(rng, extent, cuts, -0.22, 0.18)
    return jnp.clip(spiked(drawn, jax.random.fold_in(rng, 3), *heavy), -reach, reach).astype(held_as)


def setup_inputs(seed: int = 0) -> dict:
    seeds = jax.random.split(jax.random.key(seed), 5)
    grad_out = bell_draw_with(seeds[0], (SEQ, C), 1.0, 6.0, ((0, 16), (1, 32)), (0, 1, 32, 2.75))
    conv_input = scatter_about(seeds[1], (SEQ, C), 1.0, 6.0, ((0, 16), (1, 32)))
    residues = scatter_about(seeds[2], (FG, M), 0.02, 0.12, (), jnp.float32)
    log_rate = draw_log_rate(jax.random.fold_in(seeds[4], 71), 0)
    return dict(grad_out=grad_out, conv_input=conv_input, residues=residues, log_rate=log_rate)


def reference(grad_out, conv_input, residues, log_rate):
    seqlen = SEQ
    rate = jnp.exp(log_rate)
    lags = jnp.arange(seqlen, dtype=jnp.float32)
    group = 256

    def one_group(index):
        ids = (index * group + jnp.arange(group, dtype=jnp.int32)) % FG
        rate_g = rate[ids]
        resid_g = residues[ids]
        decay = jnp.exp(-rate_g[:, :, None] * lags)
        filt = jnp.einsum('cm,cmt->ct', resid_g, decay)
        spectrum = jnp.fft.rfft(filt, n=2 * seqlen, axis=1)
        start = (index * group).astype(jnp.int32)
        upstream = lax.dynamic_slice_in_dim(grad_out, start, group, 1).astype(jnp.float32).T
        inputs = lax.dynamic_slice_in_dim(conv_input, start, group, 1).astype(jnp.float32).T
        flipped = jnp.fft.rfft(upstream[:, ::-1], n=2 * seqlen, axis=1)
        back = jnp.fft.irfft(flipped * spectrum, n=2 * seqlen, axis=1)[:, :seqlen][:, ::-1]
        forward = jnp.fft.rfft(upstream, n=2 * seqlen, axis=1)
        mirror = jnp.fft.rfft(inputs[:, ::-1], n=2 * seqlen, axis=1)
        corr = jnp.fft.irfft(forward * mirror, n=2 * seqlen, axis=1)[:, seqlen - 1:2 * seqlen - 1]
        plain = jnp.einsum('ct,cmt->cm', corr, decay)
        weighted = jnp.einsum('ct,cmt->cm', corr * lags, decay)
        return back.T.astype(jnp.bfloat16), plain / seqlen, -rate_g * resid_g * weighted / seqlen

    back, plain, lagged = lax.map(one_group, jnp.arange(C // group, dtype=jnp.int32))
    grad_input = back.transpose(1, 0, 2).reshape(seqlen, C)
    grad_residue = plain.reshape(C // FG, FG, M).sum(axis=0)
    grad_lograte = lagged.reshape(C // FG, FG, M).sum(axis=0)
    return grad_input, grad_residue, grad_lograte
```

```python
import functools

import jax
import jax.numpy as jnp
from jax import lax
from jax.experimental import pallas as pl
from jax.experimental.pallas import tpu as pltpu
from jax.sharding import PartitionSpec as P

LANES = 128
SUBS = 8
F32 = jnp.float32


def strided(ref, first, stride):
    return ref[pl.ds(first, SUBS, stride=stride), :]


def widen(src_ref, dst_ref):
    rows = 64

    @pl.loop(0, src_ref.shape[0] // rows)
    def _(i):
        at = pl.ds(pl.multiple_of(i * rows, rows), rows)
        dst_ref[at, :] = src_ref[at, :].astype(F32)


def summary_kernel(seqlen, g_ref, x_ref, lr_ref, rs_ref, send_ref, state_ref, gs, xs, acc):
    half = pl.program_id(0)
    tokens = g_ref.shape[0]
    run = tokens // SUBS
    modes = lr_ref.shape[0]
    widen(g_ref, gs)
    widen(x_ref, xs)
    rate = jnp.exp(lr_ref[...])
    zero = rate * 0.0
    some = 4
    for first in range(0, modes, some):
        decay = [
            jnp.broadcast_to(jnp.exp(-rate[m : m + 1]), (SUBS, LANES)) for m in range(first, first + some)
        ]

        def step(i, carry):
            back = run - 1 - i
            g = strided(gs, back, run)
            xb = strided(xs, back, run)
            xf = strided(xs, i, run)
            out = []
            for a, (w, q, r, l, n, f) in zip(decay, carry):
                t = a * w
                q = a * q + t
                w = t + g
                r = r + xb * w
                l = l + xb * q
                n = a * (n + xf)
                f = a * f + n
                out.append((w, q, r, l, n, f))
            return tuple(out)

        sums = lax.fori_loop(0, run, step, ((zero,) * 6,) * some, unroll=4)
        for k in range(some):
            rows = slice((first + k) * SUBS, (first + k + 1) * SUBS)
            for j in range(6):
                acc[j, rows, :] = sums[k][j]

    leap = jnp.exp(-float(run) * rate)
    w = q = res = lag = zero
    for c in range(SUBS - 1, -1, -1):
        wc, qc, rc, lc, nc, fc = (strided(acc.at[j], c, SUBS) for j in range(6))
        state_ref[pl.ds(c, SUBS, stride=SUBS), :] = w
        res = res + rc + nc * w
        lag = lag + lc + nc * q + fc * w
        q = qc + leap * (q + float(run) * w)
        w = wc + leap * w
    near = far = zero
    for c in range(SUBS):
        nc, fc = strided(acc.at[4], c, SUBS), strided(acc.at[5], c, SUBS)
        far = fc + leap * (far + float(run) * near)
        near = nc + leap * near

    span = jnp.exp(-float(tokens) * rate)
    factor = -rate * rs_ref[...] / seqlen
    parts = (w, q, near, far, res, lag, span, factor)
    slot = lax.broadcasted_iota(jnp.int32, (SUBS, LANES), 1) // 16
    for d in range(8):
        packed = zero
        for j, part in enumerate(parts):
            shift = ((j - d) * 16) % LANES
            moved = pltpu.roll(part, shift, 1) if shift else part
            packed = jnp.where(slot == j, moved, packed)
        send_ref[half * 8 + d, 16:24, :] = packed
    for d in range(16):
        send_ref[d, pl.ds(pl.multiple_of(half * 8, 8), 8), :] = w


def join_kernel(seqlen, tokens, got_ref, send_ref):
    blocks = got_ref.shape[0]

    def part(k, j):
        tile = got_ref[k, :, :]
        return pltpu.roll(tile, (-16 * j) % LANES, 1) if j else tile

    zero = jnp.zeros((SUBS, LANES), F32)
    w = q = res = lag = zero
    span = part(0, 6)
    for k in range(blocks - 1, -1, -1):
        wk, qk, nk, fk, rk, lk = (part(k, j) for j in range(6))
        res = res + rk + nk * w
        lag = lag + lk + nk * q + fk * w
        q = qk + span * (q + float(tokens) * w)
        w = wk + span * w
    lane = lax.broadcasted_iota(jnp.int32, (SUBS, LANES), 1)
    res = jnp.where(lane < 16, res * (1.0 / seqlen), 0.0)
    lag = pltpu.roll(jnp.where(lane < 16, lag * part(0, 7), 0.0), 16, 1)
    tile = res + lag
    for d in range(send_ref.shape[0]):
        send_ref[d, :, :] = tile


def input_kernel(tokens, me_ref, g_ref, lr_ref, rs_ref, got_ref, state_ref, out_ref, gs, os):
    run = tokens // SUBS
    modes = lr_ref.shape[0]
    widen(g_ref, gs)
    rate = jnp.exp(lr_ref[...])
    span = jnp.exp(-float(tokens) * rate)
    me = me_ref[0]
    enter = jnp.zeros((SUBS, LANES), F32)
    for k in range(got_ref.shape[0] - 1, 0, -1):
        enter = jnp.where(k > me, got_ref[k, :, :] + span * enter, enter)
    after = (SUBS - 1) - lax.broadcasted_iota(jnp.int32, (SUBS, LANES), 0)
    runs_left = after.astype(F32) * float(run)
    decay, resid, start = [], [], []
    for m in range(modes):
        rm = jnp.broadcast_to(rate[m : m + 1], (SUBS, LANES))
        decay.append(jnp.exp(-rm))
        resid.append(jnp.broadcast_to(rs_ref[m : m + 1, :], (SUBS, LANES)))
        start.append(state_ref[m * SUBS : (m + 1) * SUBS, :] + jnp.exp(-rm * runs_left) * enter[m : m + 1])

    def step(i, carry):
        back = run - 1 - i
        g = strided(gs, back, run)
        carry = tuple(a * w + g for a, w in zip(decay, carry))
        terms = [r * w for r, w in zip(resid, carry)]
        while len(terms) > 1:
            terms = [a + b for a, b in zip(terms[::2], terms[1::2])]
        os[pl.ds(back, SUBS, stride=run), :] = terms[0]
        return carry

    lax.fori_loop(0, run, step, tuple(start), unroll=4)
    rows = 64

    @pl.loop(0, tokens // rows)
    def _(i):
        at = pl.ds(pl.multiple_of(i * rows, rows), rows)
        out_ref[at, :] = os[at, :].astype(out_ref.dtype)


def total_kernel(got_ref, res_ref, lag_ref):
    total = got_ref[0, :, :]
    for k in range(1, got_ref.shape[0]):
        total = total + got_ref[k, :, :]
    res_ref[...] = total[:, :16]
    lag_ref[...] = total[:, 16:32]


def on_device(grad_out, conv_input, residues, log_rate):
    n_context, n_data = lax.axis_size("ctx"), lax.axis_size("dp")
    tokens, chans = grad_out.shape
    filters, modes = residues.shape
    seqlen = tokens * n_context
    halves = chans // LANES
    rate_rows, resid_rows = log_rate.T, residues.T
    column = lambda h: (0, h)
    big = pl.BlockSpec((tokens, LANES), column)
    small = pl.BlockSpec((modes, LANES), column)
    states = pl.BlockSpec((modes * SUBS, LANES), column)
    params = pltpu.CompilerParams(vmem_limit_bytes=32 * 1024 * 1024)

    send, state = pl.pallas_call(
        functools.partial(summary_kernel, float(seqlen)),
        grid=(halves,),
        in_specs=[big, big, small, small],
        out_specs=[pl.BlockSpec((n_context, 24, LANES), lambda h: (0, 0, 0)), states],
        out_shape=[
            jax.ShapeDtypeStruct((n_context, 24, LANES), F32),
            jax.ShapeDtypeStruct((modes * SUBS, chans), F32),
        ],
        scratch_shapes=[
            pltpu.VMEM((tokens, LANES), F32),
            pltpu.VMEM((tokens, LANES), F32),
            pltpu.VMEM((6, modes * SUBS, LANES), F32),
        ],
        compiler_params=params,
        name="summary",
    )(grad_out, conv_input, rate_rows, resid_rows)

    got = lax.all_to_all(send, "ctx", split_axis=0, concat_axis=0, tiled=True)

    shares = pl.pallas_call(
        functools.partial(join_kernel, float(seqlen), tokens),
        grid=(1,),
        in_specs=[pl.BlockSpec((n_context, SUBS, LANES), lambda h: (0, 2, 0))],
        out_specs=pl.BlockSpec((n_data, SUBS, LANES), lambda h: (0, 0, 0)),
        out_shape=jax.ShapeDtypeStruct((n_data, SUBS, LANES), F32),
        compiler_params=params,
        name="join",
    )(got)

    shared = lax.all_to_all(shares, "dp", split_axis=0, concat_axis=0, tiled=True)

    me = lax.axis_index("ctx").astype(jnp.int32).reshape(1)
    grad_input = pl.pallas_call(
        functools.partial(input_kernel, tokens),
        grid=(halves,),
        in_specs=[
            pl.BlockSpec(memory_space=pltpu.SMEM),
            big,
            small,
            small,
            pl.BlockSpec((n_context, SUBS, LANES), lambda h: (0, h, 0)),
            states,
        ],
        out_specs=big,
        out_shape=jax.ShapeDtypeStruct((tokens, chans), jnp.bfloat16),
        scratch_shapes=[pltpu.VMEM((tokens, LANES), F32), pltpu.VMEM((tokens, LANES), F32)],
        compiler_params=params,
        cost_estimate=pl.CostEstimate(
            flops=4 * tokens * chans * modes, bytes_accessed=4 * tokens * chans, transcendentals=0
        ),
        name="input_gradient",
    )(me, grad_out, rate_rows, resid_rows, got, state)

    whole = pl.BlockSpec((modes, 16), lambda h: (0, 0))
    grad_residue, grad_lograte = pl.pallas_call(
        total_kernel,
        grid=(1,),
        in_specs=[pl.BlockSpec((n_data, SUBS, LANES), lambda h: (0, 0, 0))],
        out_specs=[whole, whole],
        out_shape=[jax.ShapeDtypeStruct((modes, 16), F32)] * 2,
        compiler_params=params,
        name="total",
    )(shared)
    return grad_input, grad_residue.T, grad_lograte.T


def solution(mesh):
    in_specs = (P("ctx", "dp"), P("ctx", "dp"), P(), P())
    out_specs = (P("ctx", "dp"), P("ctx", None), P("ctx", None))
    return jax.shard_map(
        on_device, mesh=mesh, in_specs=in_specs, out_specs=out_specs, check_vma=False
    )
```

```python
import functools

import jax
import jax.numpy as jnp
from jax import lax
from jax.experimental import pallas as pl
from jax.experimental.pallas import tpu as pltpu
from jax.sharding import PartitionSpec as P

LANES = 128
SUBS = 8
OWN = 16
STEP = 4
SOME = 4
F32 = jnp.float32
BF16 = jnp.bfloat16
VMEM = pl.BlockSpec(memory_space=pltpu.VMEM)
HBM = pl.BlockSpec(memory_space=pltpu.HBM)
SMEM = pl.BlockSpec(memory_space=pltpu.SMEM)


def interleave(src_ref, dst_ref, base):
    run = src_ref.shape[0] // SUBS

    @pl.loop(0, run // 16)
    def _(i):
        for c in range(SUBS):
            rows = src_ref[pl.ds(pl.multiple_of(c * run + i * 16, 16), 16), :]
            dst_ref[pl.ds(base + i * (16 * SUBS) + c, 16, stride=SUBS), :] = rows.astype(F32)


def step_of(ref, base, b):
    size = STEP * SUBS
    rows = ref[pl.ds(pl.multiple_of(base + b * size, size), size), :]
    return [rows[j * SUBS : (j + 1) * SUBS] for j in range(STEP)]


def summary_kernel(
    seqlen, me_ref, g_hbm, x_hbm, lr_hbm, rs_hbm,
    send_ref, state_ref, wide_ref, own_ref,
    gb, xb, lr_ref, rs_ref, xs, acc, ws, packs, sems,
):
    tokens = g_hbm.shape[0]
    halves = g_hbm.shape[1] // LANES
    run = tokens // SUBS
    steps = run // STEP
    modes = lr_hbm.shape[0]

    def column(hbm, buf, half, sem):
        return pltpu.make_async_copy(hbm.at[:, pl.ds(half * LANES, LANES)], buf.at[half], sem)

    small = [
        column(hbm, buf, half, sems.at[2 * i + half])
        for i, (hbm, buf) in enumerate(((lr_hbm, lr_ref), (rs_hbm, rs_ref)))
        for half in range(halves)
    ]
    large = [
        [column(g_hbm, gb, half, sems.at[4 + half]), column(x_hbm, xb, half, sems.at[6 + half])]
        for half in range(halves)
    ]
    for copy in large[0] + small + large[1]:
        copy.start()
    for copy in small:
        copy.wait()

    for half in range(halves):
        base = half * tokens
        rate = jnp.exp(lr_ref[half])
        zero = rate * 0.0
        for copy in large[half]:
            copy.wait()
        interleave(gb.at[half], wide_ref, base)
        interleave(xb.at[half], xs, 0)

        def near_lags(i, carry):
            g0, g1, g2, g3 = step_of(wide_ref, base, i)
            x0, x1, x2, x3 = step_of(xs, 0, i)
            c0, c1, c2, c3 = carry
            return (
                c0 + ((g0 * x0 + g1 * x1) + (g2 * x2 + g3 * x3)),
                c1 + ((g1 * x0 + g2 * x1) + g3 * x2),
                c2 + (g2 * x0 + g3 * x1),
                c3 + g3 * x0,
            )

        c0, c1, c2, c3 = lax.fori_loop(0, steps, near_lags, (zero,) * 4, unroll=4)

        for first in range(0, modes, SOME):
            rows = [jnp.broadcast_to(rate[m : m + 1], (SUBS, LANES)) for m in range(first, first + SOME)]
            decay = [jnp.exp(-r) for r in rows]
            leap = [jnp.exp(-float(STEP) * r) for r in rows]

            def step(i, carry):
                b = steps - 1 - i
                g0, g1, g2, g3 = step_of(wide_ref, base, b)
                x0, x1, x2, x3 = step_of(xs, 0, b)
                out = []
                for a, a4, (w, q, r, l, n, s, e, p) in zip(decay, leap, carry):
                    y0 = a * x0
                    y1 = x1 + y0
                    y2 = x2 + a * y1
                    v = x3 + a * y2
                    dv = a * (y2 + a * (y1 + y0))
                    r = r + v * w
                    l = l + (v * q + dv * w)
                    n = n + p * v
                    s = s + n
                    e = e + p * dv
                    p = p * a4
                    h = a * g3
                    t2 = g2 + h
                    t1 = g1 + a * t2
                    u = g0 + a * t1
                    du = a * (t1 + a * (t2 + h))
                    z = a4 * w
                    q = (du + a4 * q) + float(STEP) * z
                    w = u + z
                    out.append((w, q, r, l, n, s, e, p))
                return tuple(out)

            start = (zero,) * 7 + (zero + 1.0,)
            sums = lax.fori_loop(0, steps, step, (start,) * SOME, unroll=8)
            for k in range(SOME):
                w, q, r, l, n, s, e, _ = sums[k]
                a = decay[k]
                k1, k2, k3 = a * c1, a * a * c2, a * a * a * c3
                values = (
                    w,
                    q,
                    a * r + (c0 + k1) + (k2 + k3),
                    a * (l + r) + k1 + 2.0 * k2 + 3.0 * k3,
                    a * n,
                    a * (n + e + float(STEP) * (float(steps) * n - s)),
                )
                for j in range(6):
                    acc[j, (first + k) * SUBS : (first + k + 1) * SUBS, :] = values[j]

        def of_run(j, c):
            return acc[j, pl.ds(c, modes, stride=SUBS), :]

        leap = jnp.exp(-float(run) * rate)
        w = q = res = lag = zero
        for c in range(SUBS - 1, -1, -1):
            wc, qc, rc, lc, nc, fc = (of_run(j, c) for j in range(6))
            state_ref[half, pl.ds(c, modes, stride=SUBS), :] = w
            res = res + rc + nc * w
            lag = lag + lc + nc * q + fc * w
            z = leap * w
            q = qc + leap * q + float(run) * z
            w = wc + z
        near = far = zero
        for c in range(SUBS):
            z = leap * near
            far = of_run(5, c) + leap * far + float(run) * z
            near = of_run(4, c) + z
        state_ref[half, modes * SUBS : modes * SUBS + modes, :] = rate
        state_ref[half, modes * SUBS + modes : modes * SUBS + 2 * modes, :] = rs_ref[half]

        ws[half * SUBS : (half + 1) * SUBS, :] = w
        res_high, lag_high = res.astype(BF16).astype(F32), lag.astype(BF16).astype(F32)
        parts = (w, q, near, far, res_high, lag_high, res - res_high, lag - lag_high)
        slot = lax.broadcasted_iota(jnp.int32, (SUBS, LANES), 1) // OWN
        for d in range(LANES // OWN):
            packed = zero
            for j, part in enumerate(parts):
                shift = ((j - d) * OWN) % LANES
                packed = jnp.where(slot == j, pltpu.roll(part, shift, 1) if shift else part, packed)
            packs[half * (LANES // OWN) + d, :, :] = packed

    ahead = ws[...]
    for d in range(send_ref.shape[0]):
        send_ref[d, :, :] = jnp.concatenate([ahead, packs[d]], axis=0).astype(BF16)

    me = me_ref[0]
    slots = LANES // OWN
    upper = me >= slots
    shift = jnp.where(me % slots == 0, 0, LANES - (me % slots) * OWN)
    rate = jnp.exp(pltpu.roll(jnp.where(upper, lr_ref[1], lr_ref[0]), shift, 1))
    resid = pltpu.roll(jnp.where(upper, rs_ref[1], rs_ref[0]), shift, 1)
    own_ref[0:SUBS, :] = jnp.exp(-float(tokens) * rate)
    own_ref[SUBS : 2 * SUBS, :] = -rate * resid * (1.0 / seqlen)


def join_kernel(seqlen, tokens, got_ref, own_ref, send_ref):
    blocks = got_ref.shape[0]

    def slot(tile, j):
        return pltpu.roll(tile, LANES - OWN * j, 1)

    span = own_ref[0:SUBS, :]
    w = q = res = lag = every = jnp.zeros((SUBS, LANES), F32)
    for k in range(blocks - 1, -1, -1):
        tile = got_ref[k, :, :].astype(F32)[2 * SUBS : 3 * SUBS]
        every = every + tile
        near = slot(tile, 2)
        res = res + near * w
        lag = lag + near * q + slot(tile, 3) * w
        z = span * w
        q = slot(tile, 1) + span * q + float(tokens) * z
        w = tile + z
    res = (res + (slot(every, 4) + slot(every, 6))) * (1.0 / seqlen)
    lag = (lag + (slot(every, 5) + slot(every, 7))) * own_ref[SUBS : 2 * SUBS, :]
    lane = lax.broadcasted_iota(jnp.int32, (SUBS, LANES), 1)

    def in_a_row(tile):
        tile = pltpu.roll(jnp.where(lane < OWN, tile, 0.0), 0, 1, stride=OWN, stride_axis=0)
        return jnp.sum(tile, axis=0, keepdims=True)

    rows = jnp.concatenate([in_a_row(res), in_a_row(lag)], axis=0)
    send_ref[...] = jnp.broadcast_to(rows[None], send_ref.shape)


def input_kernel(tokens, me_ref, got_ref, state_ref, wide_ref, out_hbm, os, ob, sems):
    run = tokens // SUBS
    steps = run // STEP
    halves = state_ref.shape[0]
    modes = SUBS
    me = me_ref[0]
    rates = [state_ref[half, modes * SUBS : modes * SUBS + modes, :] for half in range(halves)]
    span = jnp.exp(-float(tokens) * jnp.concatenate(rates, axis=0))
    enter = jnp.zeros_like(span)
    for k in range(got_ref.shape[0] - 1, 0, -1):
        tile = got_ref[k, :, :].astype(F32)[: halves * modes]
        enter = jnp.where(k > me, tile + span * enter, enter)
    after = (SUBS - 1) - lax.broadcasted_iota(jnp.int32, (SUBS, LANES), 0)
    runs_left = after.astype(F32) * float(run)

    def writeback(half):
        return pltpu.make_async_copy(ob.at[half], out_hbm.at[:, pl.ds(half * LANES, LANES)], sems.at[half])

    for half in range(halves):
        base = half * tokens
        decay, resid, start = [], [], []
        for m in range(modes):
            at = modes * SUBS + m
            rm = jnp.broadcast_to(state_ref[half, at : at + 1, :], (SUBS, LANES))
            decay.append(jnp.exp(-rm))
            resid.append(jnp.broadcast_to(state_ref[half, at + modes : at + modes + 1, :], (SUBS, LANES)))
            row = half * modes + m
            start.append(
                state_ref[half, m * SUBS : (m + 1) * SUBS, :] + jnp.exp(-rm * runs_left) * enter[row : row + 1]
            )

        def step(i, carry):
            b = steps - 1 - i
            values = step_of(wide_ref, base, b)
            sums = [None] * STEP
            for j in range(STEP - 1, -1, -1):
                carry = tuple(a * w + values[j] for a, w in zip(decay, carry))
                terms = [r * w for r, w in zip(resid, carry)]
                while len(terms) > 1:
                    terms = [a + b for a, b in zip(terms[::2], terms[1::2])]
                sums[j] = terms[0]
            size = STEP * SUBS
            os[pl.ds(pl.multiple_of(b * size, size), size), :] = jnp.concatenate(sums, axis=0)
            return carry

        lax.fori_loop(0, steps, step, tuple(start), unroll=2)

        @pl.loop(0, run // 16)
        def _(i):
            for c in range(SUBS):
                rows = os[pl.ds(i * (16 * SUBS) + c, 16, stride=SUBS), :]
                ob[half, pl.ds(pl.multiple_of(c * run + i * 16, 16), 16), :] = rows.astype(BF16)

        writeback(half).start()
    for half in range(halves):
        writeback(half).wait()


def total_kernel(got_ref, res_ref, lag_ref):
    total = got_ref[0, :, :]
    for k in range(1, got_ref.shape[0]):
        total = total + got_ref[k, :, :]
    mode = lax.broadcasted_iota(jnp.int32, (SUBS, LANES), 0)
    for j, out in enumerate((res_ref, lag_ref)):
        row = jnp.broadcast_to(total[j : j + 1], (SUBS, LANES))
        tile = row
        for m in range(1, SUBS):
            tile = jnp.where(mode == m, pltpu.roll(row, LANES - OWN * m, 1), tile)
        out[...] = tile[:, :OWN]


def on_device(grad_out, conv_input, residues, log_rate):
    n_context, n_data = lax.axis_size("ctx"), lax.axis_size("dp")
    tokens, chans = grad_out.shape
    modes = residues.shape[1]
    seqlen = tokens * n_context
    halves = chans // LANES
    me = lax.axis_index("ctx").astype(jnp.int32).reshape(1)
    params = pltpu.CompilerParams(vmem_limit_bytes=24 * 1024 * 1024)

    send, state, wide, own = pl.pallas_call(
        functools.partial(summary_kernel, float(seqlen)),
        in_specs=[SMEM, HBM, HBM, HBM, HBM],
        out_specs=[VMEM, VMEM, VMEM, VMEM],
        out_shape=[
            jax.ShapeDtypeStruct((n_context, 3 * SUBS, LANES), BF16),
            jax.ShapeDtypeStruct((halves, modes * SUBS + 2 * modes, LANES), F32),
            jax.ShapeDtypeStruct((halves * tokens, LANES), F32),
            jax.ShapeDtypeStruct((2 * SUBS, LANES), F32),
        ],
        scratch_shapes=[
            pltpu.VMEM((halves, tokens, LANES), BF16),
            pltpu.VMEM((halves, tokens, LANES), BF16),
            pltpu.VMEM((halves, modes, LANES), F32),
            pltpu.VMEM((halves, modes, LANES), F32),
            pltpu.VMEM((tokens, LANES), F32),
            pltpu.VMEM((6, modes * SUBS, LANES), F32),
            pltpu.VMEM((halves * modes, LANES), F32),
            pltpu.VMEM((n_context, modes, LANES), F32),
            pltpu.SemaphoreType.DMA((8,)),
        ],
        compiler_params=params,
        name="summary",
    )(me, *(
        pltpu.with_memory_space_constraint(array, pltpu.HBM)
        for array in (grad_out, conv_input, log_rate.T, residues.T)
    ))

    got = lax.all_to_all(send, "ctx", split_axis=0, concat_axis=0, tiled=True)

    shares = pl.pallas_call(
        functools.partial(join_kernel, float(seqlen), tokens),
        in_specs=[VMEM, VMEM],
        out_specs=VMEM,
        out_shape=jax.ShapeDtypeStruct((n_data, 2, LANES), F32),
        compiler_params=params,
        name="join",
    )(got, own)

    shared = lax.all_to_all(shares, "dp", split_axis=0, concat_axis=0, tiled=True)

    grad_input = pl.pallas_call(
        functools.partial(input_kernel, tokens),
        in_specs=[SMEM, VMEM, VMEM, VMEM],
        out_specs=HBM,
        out_shape=jax.ShapeDtypeStruct((tokens, chans), BF16),
        scratch_shapes=[
            pltpu.VMEM((tokens, LANES), F32),
            pltpu.VMEM((halves, tokens, LANES), BF16),
            pltpu.SemaphoreType.DMA((2,)),
        ],
        compiler_params=params,
        cost_estimate=pl.CostEstimate(
            flops=4 * tokens * chans * modes, bytes_accessed=4 * tokens * chans, transcendentals=0
        ),
        name="input_gradient",
    )(me, got, state, wide)

    grad_residue, grad_lograte = pl.pallas_call(
        total_kernel,
        in_specs=[VMEM],
        out_specs=[VMEM, VMEM],
        out_shape=[jax.ShapeDtypeStruct((modes, OWN), F32)] * 2,
        compiler_params=params,
        name="total",
    )(shared)
    return grad_input, grad_residue.T, grad_lograte.T


def solution(mesh):
    in_specs = (P("ctx", "dp"), P("ctx", "dp"), P(), P())
    out_specs = (P("ctx", "dp"), P("ctx", None), P("ctx", None))
    return jax.shard_map(
        on_device, mesh=mesh, in_specs=in_specs, out_specs=out_specs, check_vma=False
    )
```

```python
import functools

import jax
import jax.numpy as jnp
from jax import lax
from jax.experimental import pallas as pl
from jax.experimental.pallas import tpu as pltpu
from jax.sharding import PartitionSpec as P

LANES = 128
SUBS = 8
OWN = 16
STEP = 4
SOME = 4
CTX_ORDER = [10, 0, 1, 3, 2, 4, 12, 5, 7, 13, 15, 6, 14, 8, 9, 11]
DP_ORDER = [21, 22, 23, 24, 25, 26, 27, 28, 29, 30, 31, 0, 1, 2, 3, 4, 5, 6, 7, 8, 9, 10, 11, 12, 13, 14, 15, 16, 17, 18, 19, 20]
F32 = jnp.float32
BF16 = jnp.bfloat16
VMEM = pl.BlockSpec(memory_space=pltpu.VMEM)
HBM = pl.BlockSpec(memory_space=pltpu.HBM)
SMEM = pl.BlockSpec(memory_space=pltpu.SMEM)


def interleave(src_ref, dst_ref, base):
    run = src_ref.shape[0] // SUBS

    @pl.loop(0, run // 16)
    def _(i):
        for c in range(SUBS):
            rows = src_ref[pl.ds(pl.multiple_of(c * run + i * 16, 16), 16), :]
            dst_ref[pl.ds(base + i * (16 * SUBS) + c, 16, stride=SUBS), :] = rows.astype(F32)


def step_of(ref, base, b):
    size = STEP * SUBS
    rows = ref[pl.ds(pl.multiple_of(base + b * size, size), size), :]
    return [rows[j * SUBS : (j + 1) * SUBS] for j in range(STEP)]


def summary_kernel(
    seqlen, me_ref, g_hbm, x_hbm, lr_hbm, rs_hbm,
    send_ref, state_ref, wide_ref, own_ref,
    gb, xb, lr_ref, rs_ref, xs, acc, ws, packs, sems,
):
    tokens = g_hbm.shape[0]
    halves = g_hbm.shape[1] // LANES
    run = tokens // SUBS
    steps = run // STEP
    modes = lr_hbm.shape[0]

    def column(hbm, buf, half, sem):
        return pltpu.make_async_copy(hbm.at[:, pl.ds(half * LANES, LANES)], buf.at[half], sem)

    small = [
        column(hbm, buf, half, sems.at[2 * i + half])
        for i, (hbm, buf) in enumerate(((lr_hbm, lr_ref), (rs_hbm, rs_ref)))
        for half in range(halves)
    ]
    large = [
        [column(g_hbm, gb, half, sems.at[4 + half]), column(x_hbm, xb, half, sems.at[6 + half])]
        for half in range(halves)
    ]
    for copy in large[0] + small + large[1]:
        copy.start()
    for copy in small:
        copy.wait()

    for half in range(halves):
        base = half * tokens
        rate = jnp.exp(lr_ref[half])
        zero = rate * 0.0
        for copy in large[half]:
            copy.wait()
        interleave(gb.at[half], wide_ref, base)
        interleave(xb.at[half], xs, 0)

        def near_lags(i, carry):
            g0, g1, g2, g3 = step_of(wide_ref, base, i)
            x0, x1, x2, x3 = step_of(xs, 0, i)
            c0, c1, c2, c3 = carry
            return (
                c0 + ((g0 * x0 + g1 * x1) + (g2 * x2 + g3 * x3)),
                c1 + ((g1 * x0 + g2 * x1) + g3 * x2),
                c2 + (g2 * x0 + g3 * x1),
                c3 + g3 * x0,
            )

        c0, c1, c2, c3 = lax.fori_loop(0, steps, near_lags, (zero,) * 4, unroll=4)

        for first in range(0, modes, SOME):
            rows = [jnp.broadcast_to(rate[m : m + 1], (SUBS, LANES)) for m in range(first, first + SOME)]
            decay = [jnp.exp(-r) for r in rows]
            leap = [jnp.exp(-float(STEP) * r) for r in rows]

            def step(i, carry):
                b = steps - 1 - i
                g0, g1, g2, g3 = step_of(wide_ref, base, b)
                x0, x1, x2, x3 = step_of(xs, 0, b)
                out = []
                for a, a4, (w, q, r, l, n, s, e, p) in zip(decay, leap, carry):
                    y0 = a * x0
                    y1 = x1 + y0
                    y2 = x2 + a * y1
                    v = x3 + a * y2
                    dv = a * (y2 + a * (y1 + y0))
                    r = r + v * w
                    l = l + (v * q + dv * w)
                    n = n + p * v
                    s = s + n
                    e = e + p * dv
                    p = p * a4
                    h = a * g3
                    t2 = g2 + h
                    t1 = g1 + a * t2
                    u = g0 + a * t1
                    du = a * (t1 + a * (t2 + h))
                    z = a4 * w
                    q = (du + a4 * q) + float(STEP) * z
                    w = u + z
                    out.append((w, q, r, l, n, s, e, p))
                return tuple(out)

            start = (zero,) * 7 + (zero + 1.0,)
            sums = lax.fori_loop(0, steps, step, (start,) * SOME, unroll=8)
            for k in range(SOME):
                w, q, r, l, n, s, e, _ = sums[k]
                a = decay[k]
                k1, k2, k3 = a * c1, a * a * c2, a * a * a * c3
                values = (
                    w,
                    q,
                    a * r + (c0 + k1) + (k2 + k3),
                    a * (l + r) + k1 + 2.0 * k2 + 3.0 * k3,
                    a * n,
                    a * (n + e + float(STEP) * (float(steps) * n - s)),
                )
                for j in range(6):
                    acc[j, (first + k) * SUBS : (first + k + 1) * SUBS, :] = values[j]

        def of_run(j, c):
            return acc[j, pl.ds(c, modes, stride=SUBS), :]

        leap = jnp.exp(-float(run) * rate)
        w = q = res = lag = zero
        for c in range(SUBS - 1, -1, -1):
            wc, qc, rc, lc, nc, fc = (of_run(j, c) for j in range(6))
            state_ref[half, pl.ds(c, modes, stride=SUBS), :] = w
            res = res + rc + nc * w
            lag = lag + lc + nc * q + fc * w
            z = leap * w
            q = qc + leap * q + float(run) * z
            w = wc + z
        near = far = zero
        for c in range(SUBS):
            z = leap * near
            far = of_run(5, c) + leap * far + float(run) * z
            near = of_run(4, c) + z
        state_ref[half, modes * SUBS : modes * SUBS + modes, :] = rate
        state_ref[half, modes * SUBS + modes : modes * SUBS + 2 * modes, :] = rs_ref[half]

        ws[half * SUBS : (half + 1) * SUBS, :] = w
        res_high, lag_high = res.astype(BF16).astype(F32), lag.astype(BF16).astype(F32)
        parts = (w, q, near, far, res_high, lag_high, res - res_high, lag - lag_high)
        slot = lax.broadcasted_iota(jnp.int32, (SUBS, LANES), 1) // OWN
        for d in range(LANES // OWN):
            packed = zero
            for j, part in enumerate(parts):
                shift = ((j - d) * OWN) % LANES
                packed = jnp.where(slot == j, pltpu.roll(part, shift, 1) if shift else part, packed)
            packs[half * (LANES // OWN) + d, :, :] = packed

    ahead = ws[...]
    for place, d in enumerate(CTX_ORDER):
        send_ref[place, :, :] = jnp.concatenate([ahead, packs[d]], axis=0).astype(BF16)

    me = me_ref[0]
    slots = LANES // OWN
    upper = me >= slots
    shift = jnp.where(me % slots == 0, 0, LANES - (me % slots) * OWN)
    rate = jnp.exp(pltpu.roll(jnp.where(upper, lr_ref[1], lr_ref[0]), shift, 1))
    resid = pltpu.roll(jnp.where(upper, rs_ref[1], rs_ref[0]), shift, 1)
    own_ref[0:SUBS, :] = jnp.exp(-float(tokens) * rate)
    own_ref[SUBS : 2 * SUBS, :] = -rate * resid * (1.0 / seqlen)


def join_kernel(seqlen, tokens, got_ref, own_ref, send_ref):
    blocks = got_ref.shape[0]

    def slot(tile, j):
        return pltpu.roll(tile, LANES - OWN * j, 1)

    span = own_ref[0:SUBS, :]
    w = q = res = lag = every = jnp.zeros((SUBS, LANES), F32)
    for k in range(blocks - 1, -1, -1):
        tile = got_ref[CTX_ORDER.index(k), :, :].astype(F32)[2 * SUBS : 3 * SUBS]
        every = every + tile
        near = slot(tile, 2)
        res = res + near * w
        lag = lag + near * q + slot(tile, 3) * w
        z = span * w
        q = slot(tile, 1) + span * q + float(tokens) * z
        w = tile + z
    res = (res + (slot(every, 4) + slot(every, 6))) * (1.0 / seqlen)
    lag = (lag + (slot(every, 5) + slot(every, 7))) * own_ref[SUBS : 2 * SUBS, :]
    lane = lax.broadcasted_iota(jnp.int32, (SUBS, LANES), 1)

    def in_a_row(tile):
        tile = pltpu.roll(jnp.where(lane < OWN, tile, 0.0), 0, 1, stride=OWN, stride_axis=0)
        return jnp.sum(tile, axis=0, keepdims=True)

    rows = jnp.concatenate([in_a_row(res), in_a_row(lag)], axis=0)
    send_ref[...] = jnp.broadcast_to(rows[None], send_ref.shape)


def input_kernel(tokens, me_ref, got_ref, state_ref, wide_ref, out_hbm, os, ob, sems):
    run = tokens // SUBS
    steps = run // STEP
    halves = state_ref.shape[0]
    modes = SUBS
    me = me_ref[0]
    rates = [state_ref[half, modes * SUBS : modes * SUBS + modes, :] for half in range(halves)]
    span = jnp.exp(-float(tokens) * jnp.concatenate(rates, axis=0))
    enter = jnp.zeros_like(span)
    for k in range(got_ref.shape[0] - 1, 0, -1):
        tile = got_ref[CTX_ORDER.index(k), :, :].astype(F32)[: halves * modes]
        enter = jnp.where(k > me, tile + span * enter, enter)
    after = (SUBS - 1) - lax.broadcasted_iota(jnp.int32, (SUBS, LANES), 0)
    runs_left = after.astype(F32) * float(run)

    def writeback(half):
        return pltpu.make_async_copy(ob.at[half], out_hbm.at[:, pl.ds(half * LANES, LANES)], sems.at[half])

    for half in range(halves):
        base = half * tokens
        decay, resid, start = [], [], []
        for m in range(modes):
            at = modes * SUBS + m
            rm = jnp.broadcast_to(state_ref[half, at : at + 1, :], (SUBS, LANES))
            decay.append(jnp.exp(-rm))
            resid.append(jnp.broadcast_to(state_ref[half, at + modes : at + modes + 1, :], (SUBS, LANES)))
            row = half * modes + m
            start.append(
                state_ref[half, m * SUBS : (m + 1) * SUBS, :] + jnp.exp(-rm * runs_left) * enter[row : row + 1]
            )

        def step(i, carry):
            b = steps - 1 - i
            values = step_of(wide_ref, base, b)
            sums = [None] * STEP
            for j in range(STEP - 1, -1, -1):
                carry = tuple(a * w + values[j] for a, w in zip(decay, carry))
                terms = [r * w for r, w in zip(resid, carry)]
                while len(terms) > 1:
                    terms = [a + b for a, b in zip(terms[::2], terms[1::2])]
                sums[j] = terms[0]
            size = STEP * SUBS
            os[pl.ds(pl.multiple_of(b * size, size), size), :] = jnp.concatenate(sums, axis=0)
            return carry

        lax.fori_loop(0, steps, step, tuple(start), unroll=2)

        @pl.loop(0, run // 16)
        def _(i):
            for c in range(SUBS):
                rows = os[pl.ds(i * (16 * SUBS) + c, 16, stride=SUBS), :]
                ob[half, pl.ds(pl.multiple_of(c * run + i * 16, 16), 16), :] = rows.astype(BF16)

        writeback(half).start()
    for half in range(halves):
        writeback(half).wait()


def total_kernel(got_ref, res_ref, lag_ref):
    total = got_ref[0, :, :]
    for k in range(1, got_ref.shape[0]):
        total = total + got_ref[k, :, :]
    mode = lax.broadcasted_iota(jnp.int32, (SUBS, LANES), 0)
    for j, out in enumerate((res_ref, lag_ref)):
        row = jnp.broadcast_to(total[j : j + 1], (SUBS, LANES))
        tile = row
        for m in range(1, SUBS):
            tile = jnp.where(mode == m, pltpu.roll(row, LANES - OWN * m, 1), tile)
        out[...] = tile[:, :OWN]


def exchange(blocks, axis, order):
    return lax.all_to_all(
        blocks, axis, split_axis=0, concat_axis=0, axis_index_groups=[order], tiled=True
    )


def on_device(grad_out, conv_input, residues, log_rate):
    n_context, n_data = lax.axis_size("ctx"), lax.axis_size("dp")
    tokens, chans = grad_out.shape
    modes = residues.shape[1]
    seqlen = tokens * n_context
    halves = chans // LANES
    me = lax.axis_index("ctx").astype(jnp.int32).reshape(1)
    params = pltpu.CompilerParams(vmem_limit_bytes=24 * 1024 * 1024)

    send, state, wide, own = pl.pallas_call(
        functools.partial(summary_kernel, float(seqlen)),
        in_specs=[SMEM, HBM, HBM, HBM, HBM],
        out_specs=[VMEM, VMEM, VMEM, VMEM],
        out_shape=[
            jax.ShapeDtypeStruct((n_context, 3 * SUBS, LANES), BF16),
            jax.ShapeDtypeStruct((halves, modes * SUBS + 2 * modes, LANES), F32),
            jax.ShapeDtypeStruct((halves * tokens, LANES), F32),
            jax.ShapeDtypeStruct((2 * SUBS, LANES), F32),
        ],
        scratch_shapes=[
            pltpu.VMEM((halves, tokens, LANES), BF16),
            pltpu.VMEM((halves, tokens, LANES), BF16),
            pltpu.VMEM((halves, modes, LANES), F32),
            pltpu.VMEM((halves, modes, LANES), F32),
            pltpu.VMEM((tokens, LANES), F32),
            pltpu.VMEM((6, modes * SUBS, LANES), F32),
            pltpu.VMEM((halves * modes, LANES), F32),
            pltpu.VMEM((n_context, modes, LANES), F32),
            pltpu.SemaphoreType.DMA((8,)),
        ],
        compiler_params=params,
        name="summary",
    )(me, *(
        pltpu.with_memory_space_constraint(array, pltpu.HBM)
        for array in (grad_out, conv_input, log_rate.T, residues.T)
    ))

    got = exchange(send, "ctx", CTX_ORDER)

    shares = pl.pallas_call(
        functools.partial(join_kernel, float(seqlen), tokens),
        in_specs=[VMEM, VMEM],
        out_specs=VMEM,
        out_shape=jax.ShapeDtypeStruct((n_data, 2, LANES), F32),
        compiler_params=params,
        name="join",
    )(got, own)

    shared = exchange(shares, "dp", DP_ORDER)

    grad_input = pl.pallas_call(
        functools.partial(input_kernel, tokens),
        in_specs=[SMEM, VMEM, VMEM, VMEM],
        out_specs=HBM,
        out_shape=jax.ShapeDtypeStruct((tokens, chans), BF16),
        scratch_shapes=[
            pltpu.VMEM((tokens, LANES), F32),
            pltpu.VMEM((halves, tokens, LANES), BF16),
            pltpu.SemaphoreType.DMA((2,)),
        ],
        compiler_params=params,
        cost_estimate=pl.CostEstimate(
            flops=4 * tokens * chans * modes, bytes_accessed=4 * tokens * chans, transcendentals=0
        ),
        name="input_gradient",
    )(me, got, state, wide)

    grad_residue, grad_lograte = pl.pallas_call(
        total_kernel,
        in_specs=[VMEM],
        out_specs=[VMEM, VMEM],
        out_shape=[jax.ShapeDtypeStruct((modes, OWN), F32)] * 2,
        compiler_params=params,
        name="total",
    )(shared)
    return grad_input, grad_residue.T, grad_lograte.T


def solution(mesh):
    in_specs = (P("ctx", "dp"), P("ctx", "dp"), P(), P())
    out_specs = (P("ctx", "dp"), P("ctx", None), P("ctx", None))
    return jax.shard_map(
        on_device, mesh=mesh, in_specs=in_specs, out_specs=out_specs, check_vma=False
    )
```

```python
import functools

import jax
import jax.numpy as jnp
from jax import lax
from jax.experimental import pallas as pl
from jax.experimental.pallas import tpu as pltpu
from jax.sharding import PartitionSpec as P

LANES = 128
SUBS = 8
OWN = 16
STEP = 4
SOME = 2
CTX_ORDER = [10, 0, 1, 3, 2, 4, 12, 5, 7, 13, 15, 6, 14, 8, 9, 11]
DP_ORDER = [21, 22, 23, 24, 25, 26, 27, 28, 29, 30, 31, 0, 1, 2, 3, 4, 5, 6, 7, 8, 9, 10, 11, 12, 13, 14, 15, 16, 17, 18, 19, 20]
F32 = jnp.float32
BF16 = jnp.bfloat16
VMEM = pl.BlockSpec(memory_space=pltpu.VMEM)
HBM = pl.BlockSpec(memory_space=pltpu.HBM)
SMEM = pl.BlockSpec(memory_space=pltpu.SMEM)


def interleave(src_ref, dst_ref, base):
    run = src_ref.shape[0] // SUBS

    @pl.loop(0, run // 16)
    def _(i):
        for c in range(SUBS):
            rows = src_ref[pl.ds(pl.multiple_of(c * run + i * 16, 16), 16), :]
            dst_ref[pl.ds(base + i * (16 * SUBS) + c, 16, stride=SUBS), :] = rows.astype(F32)


def step_of(ref, base, b):
    size = STEP * SUBS
    rows = ref[pl.ds(pl.multiple_of(base + b * size, size), size), :]
    return [rows[j * SUBS : (j + 1) * SUBS] for j in range(STEP)]


def summary_kernel(
    seqlen, me_ref, g_hbm, x_hbm, lr_hbm, rs_hbm,
    send_ref, state_ref, wide_ref, own_ref,
    gb, xb, lr_ref, rs_ref, xs, acc, sems,
):
    tokens = g_hbm.shape[0]
    halves = g_hbm.shape[1] // LANES
    run = tokens // SUBS
    steps = run // STEP
    modes = lr_hbm.shape[0]

    def column(hbm, buf, half, sem):
        return pltpu.make_async_copy(hbm.at[:, pl.ds(half * LANES, LANES)], buf.at[half], sem)

    small = [
        column(hbm, buf, half, sems.at[2 * i + half])
        for i, (hbm, buf) in enumerate(((lr_hbm, lr_ref), (rs_hbm, rs_ref)))
        for half in range(halves)
    ]
    large = [
        [column(g_hbm, gb, half, sems.at[4 + half]), column(x_hbm, xb, half, sems.at[6 + half])]
        for half in range(halves)
    ]
    for copy in large[0] + small:
        copy.start()

    def scan(half):
        base = half * tokens
        for copy, src, dst, at in zip(large[half], (gb, xb), (wide_ref, xs), (base, 0)):
            copy.wait()
            interleave(src.at[half], dst, at)
        if half == 0:
            for copy in large[1]:
                copy.start()
            for copy in small:
                copy.wait()
        rate = jnp.exp(lr_ref[half])
        zero = rate * 0.0
        for first in range(0, modes, SOME):
            rows = [jnp.broadcast_to(rate[m : m + 1], (SUBS, LANES)) for m in range(first, first + SOME)]
            decay = [jnp.exp(-r) for r in rows]
            part = [a * (1.0 / STEP) for a in decay]
            leap = [jnp.exp(-float(STEP) * r) for r in rows]

            def step(i, carry):
                b = steps - 1 - i
                g0, g1, g2, g3 = step_of(wide_ref, base, b)
                x0, x1, x2, x3 = step_of(xs, 0, b)
                out = []
                for a, a_part, a4, (w, q, r, l, n, f, p) in zip(decay, part, leap, carry):
                    y0 = a * x0
                    y1 = x1 + y0
                    y2 = x2 + a * y1
                    v = x3 + a * y2
                    dv = a_part * (y2 + a * (y1 + y0))
                    r = r + v * w
                    l = l + (v * q + dv * w)
                    n = n + p * v
                    f = f + (p * dv - n)
                    p = p * a4
                    h = a * g3
                    t2 = g2 + h
                    t1 = g1 + a * t2
                    u = g0 + a * t1
                    du = a_part * (t1 + a * (t2 + h))
                    z = a4 * w
                    q = (du + a4 * q) + z
                    w = u + z
                    out.append((w, q, r, l, n, f, p))
                if first == 0:
                    c0, c1, c2, c3 = carry[SOME]
                    out.append((
                        c0 + ((g0 * x0 + g1 * x1) + (g2 * x2 + g3 * x3)),
                        c1 + ((g1 * x0 + g2 * x1) + g3 * x2),
                        c2 + (g2 * x0 + g3 * x1),
                        c3 + g3 * x0,
                    ))
                return tuple(out)

            start = ((zero,) * 6 + (zero + 1.0,),) * SOME
            if first == 0:
                start = start + ((zero,) * 4,)
            sums = lax.fori_loop(0, steps, step, start, unroll=16)
            if first == 0:
                c0, c1, c2, c3 = sums[SOME]
            for k in range(SOME):
                w, q, r, l, n, f, _ = sums[k]
                a = decay[k]
                k1, k2, k3 = a * c1, a * a * c2, a * a * a * c3
                values = (
                    w,
                    float(STEP) * q,
                    a * r + (c0 + k1) + (k2 + k3),
                    a * (float(STEP) * l + r) + k1 + 2.0 * k2 + 3.0 * k3,
                    a * n,
                    a * (n + float(STEP) * (f + float(steps) * n)),
                )
                for j in range(6):
                    acc[half, j, (first + k) * SUBS : (first + k + 1) * SUBS, :] = values[j]

    both = range(halves)
    for half in both:
        scan(half)

    def of_run(j, c):
        return [acc[half, j, pl.ds(c, modes, stride=SUBS), :] for half in both]

    def each(rule, *columns):
        return [rule(*values) for values in zip(*columns)]

    rate = [jnp.exp(lr_ref[half]) for half in both]
    leap = each(lambda r: jnp.exp(-float(run) * r), rate)
    w = q = res = lag = near = far = each(lambda r: r * 0.0, rate)
    for i in range(SUBS):
        c = SUBS - 1 - i
        wc, qc, rc, lc, nc, fc = (of_run(j, c) for j in range(6))
        for half in both:
            state_ref[half, pl.ds(c, modes, stride=SUBS), :] = w[half]
        res = each(lambda t, r, n, w: t + r + n * w, res, rc, nc, w)
        lag = each(lambda t, l, n, f, w, q: t + l + (n * q + f * w), lag, lc, nc, fc, w, q)
        z = each(lambda a, w: a * w, leap, w)
        q = each(lambda qc, a, q, z: qc + a * q + float(run) * z, qc, leap, q, z)
        w = each(lambda wc, z: wc + z, wc, z)
        nc, fc = of_run(4, i), of_run(5, i)
        z = each(lambda a, n: a * n, leap, near)
        far = each(lambda fc, a, f, z: fc + a * f + float(run) * z, fc, leap, far, z)
        near = each(lambda nc, z: nc + z, nc, z)

    slot = lax.broadcasted_iota(jnp.int32, (SUBS, LANES), 1) // OWN
    ahead = jnp.concatenate(w, axis=0)
    for half in both:
        state_ref[half, modes * SUBS : modes * SUBS + modes, :] = rate[half]
        state_ref[half, modes * SUBS + modes : modes * SUBS + 2 * modes, :] = rs_ref[half]
        res_high, lag_high = res[half].astype(BF16).astype(F32), lag[half].astype(BF16).astype(F32)
        parts = (
            w[half], q[half], near[half], far[half],
            res_high, lag_high, res[half] - res_high, lag[half] - lag_high,
        )
        for d in range(LANES // OWN):
            packed = parts[d]
            for j, part in enumerate(parts):
                if j != d:
                    packed = jnp.where(slot == j, pltpu.roll(part, ((j - d) * OWN) % LANES, 1), packed)
            place = CTX_ORDER.index(half * (LANES // OWN) + d)
            send_ref[place, :, :] = jnp.concatenate([ahead, packed], axis=0).astype(BF16)

    me = me_ref[0]
    slots = LANES // OWN
    upper = me >= slots
    shift = jnp.where(me % slots == 0, 0, LANES - (me % slots) * OWN)
    rate = jnp.exp(pltpu.roll(jnp.where(upper, lr_ref[1], lr_ref[0]), shift, 1))
    resid = pltpu.roll(jnp.where(upper, rs_ref[1], rs_ref[0]), shift, 1)
    own_ref[0:SUBS, :] = jnp.exp(-float(tokens) * rate)
    own_ref[SUBS : 2 * SUBS, :] = -rate * resid * (1.0 / seqlen)


def join_kernel(seqlen, tokens, got_ref, own_ref, send_ref):
    blocks = got_ref.shape[0]

    def slot(tile, j):
        return pltpu.roll(tile, LANES - OWN * j, 1)

    span = own_ref[0:SUBS, :]
    w = q = res = lag = every = jnp.zeros((SUBS, LANES), F32)
    for k in range(blocks - 1, -1, -1):
        tile = got_ref[CTX_ORDER.index(k), :, :].astype(F32)[2 * SUBS : 3 * SUBS]
        every = every + tile
        near = slot(tile, 2)
        res = res + near * w
        lag = lag + near * q + slot(tile, 3) * w
        z = span * w
        q = slot(tile, 1) + span * q + float(tokens) * z
        w = tile + z
    res = (res + (slot(every, 4) + slot(every, 6))) * (1.0 / seqlen)
    lag = (lag + (slot(every, 5) + slot(every, 7))) * own_ref[SUBS : 2 * SUBS, :]
    lane = lax.broadcasted_iota(jnp.int32, (SUBS, LANES), 1)

    def in_a_row(tile):
        tile = pltpu.roll(jnp.where(lane < OWN, tile, 0.0), 0, 1, stride=OWN, stride_axis=0)
        return jnp.sum(tile, axis=0, keepdims=True)

    rows = jnp.concatenate([in_a_row(res), in_a_row(lag)], axis=0)
    send_ref[...] = jnp.broadcast_to(rows[None], send_ref.shape)


def input_kernel(tokens, me_ref, got_ref, state_ref, wide_ref, out_hbm, os, ob, sems):
    run = tokens // SUBS
    steps = run // STEP
    halves = state_ref.shape[0]
    modes = SUBS
    me = me_ref[0]
    rates = [state_ref[half, modes * SUBS : modes * SUBS + modes, :] for half in range(halves)]
    span = jnp.exp(-float(tokens) * jnp.concatenate(rates, axis=0))
    enter = jnp.zeros_like(span)
    for k in range(got_ref.shape[0] - 1, 0, -1):
        tile = got_ref[CTX_ORDER.index(k), :, :].astype(F32)[: halves * modes]
        enter = jnp.where(k > me, tile + span * enter, enter)
    after = (SUBS - 1) - lax.broadcasted_iota(jnp.int32, (SUBS, LANES), 0)
    runs_left = after.astype(F32) * float(run)

    def writeback(half):
        return pltpu.make_async_copy(ob.at[half], out_hbm.at[:, pl.ds(half * LANES, LANES)], sems.at[half])

    for half in range(halves):
        base = half * tokens
        decay, resid, start = [], [], []
        for m in range(modes):
            at = modes * SUBS + m
            rm = jnp.broadcast_to(state_ref[half, at : at + 1, :], (SUBS, LANES))
            decay.append(jnp.exp(-rm))
            resid.append(jnp.broadcast_to(state_ref[half, at + modes : at + modes + 1, :], (SUBS, LANES)))
            row = half * modes + m
            start.append(
                state_ref[half, m * SUBS : (m + 1) * SUBS, :] + jnp.exp(-rm * runs_left) * enter[row : row + 1]
            )

        def step(i, carry):
            b = steps - 1 - i
            values = step_of(wide_ref, base, b)
            sums = [None] * STEP
            for j in range(STEP - 1, -1, -1):
                carry = tuple(a * w + values[j] for a, w in zip(decay, carry))
                terms = [r * w for r, w in zip(resid, carry)]
                while len(terms) > 1:
                    terms = [a + b for a, b in zip(terms[::2], terms[1::2])]
                sums[j] = terms[0]
            size = STEP * SUBS
            os[pl.ds(pl.multiple_of(b * size, size), size), :] = jnp.concatenate(sums, axis=0)
            return carry

        lax.fori_loop(0, steps, step, tuple(start), unroll=2)

        @pl.loop(0, run // 16)
        def _(i):
            for c in range(SUBS):
                rows = os[pl.ds(i * (16 * SUBS) + c, 16, stride=SUBS), :]
                ob[half, pl.ds(pl.multiple_of(c * run + i * 16, 16), 16), :] = rows.astype(BF16)

        writeback(half).start()
    for half in range(halves):
        writeback(half).wait()


def total_kernel(got_ref, res_ref, lag_ref):
    total = got_ref[0, :, :]
    for k in range(1, got_ref.shape[0]):
        total = total + got_ref[k, :, :]
    mode = lax.broadcasted_iota(jnp.int32, (SUBS, LANES), 0)
    for j, out in enumerate((res_ref, lag_ref)):
        row = jnp.broadcast_to(total[j : j + 1], (SUBS, LANES))
        tile = row
        for m in range(1, SUBS):
            tile = jnp.where(mode == m, pltpu.roll(row, LANES - OWN * m, 1), tile)
        out[...] = tile[:, :OWN]


def exchange(blocks, axis, order):
    return lax.all_to_all(
        blocks, axis, split_axis=0, concat_axis=0, axis_index_groups=[order], tiled=True
    )


def on_device(grad_out, conv_input, residues, log_rate):
    n_context, n_data = lax.axis_size("ctx"), lax.axis_size("dp")
    tokens, chans = grad_out.shape
    modes = residues.shape[1]
    seqlen = tokens * n_context
    halves = chans // LANES
    me = lax.axis_index("ctx").astype(jnp.int32).reshape(1)
    params = pltpu.CompilerParams(vmem_limit_bytes=24 * 1024 * 1024)

    send, state, wide, own = pl.pallas_call(
        functools.partial(summary_kernel, float(seqlen)),
        in_specs=[SMEM, HBM, HBM, HBM, HBM],
        out_specs=[VMEM, VMEM, VMEM, VMEM],
        out_shape=[
            jax.ShapeDtypeStruct((n_context, 3 * SUBS, LANES), BF16),
            jax.ShapeDtypeStruct((halves, modes * SUBS + 2 * modes, LANES), F32),
            jax.ShapeDtypeStruct((halves * tokens, LANES), F32),
            jax.ShapeDtypeStruct((2 * SUBS, LANES), F32),
        ],
        scratch_shapes=[
            pltpu.VMEM((halves, tokens, LANES), BF16),
            pltpu.VMEM((halves, tokens, LANES), BF16),
            pltpu.VMEM((halves, modes, LANES), F32),
            pltpu.VMEM((halves, modes, LANES), F32),
            pltpu.VMEM((tokens, LANES), F32),
            pltpu.VMEM((halves, 6, modes * SUBS, LANES), F32),
            pltpu.SemaphoreType.DMA((8,)),
        ],
        compiler_params=params,
        name="summary",
    )(me, *(
        pltpu.with_memory_space_constraint(array, pltpu.HBM)
        for array in (grad_out, conv_input, log_rate.T, residues.T)
    ))

    got = exchange(send, "ctx", CTX_ORDER)

    shares = pl.pallas_call(
        functools.partial(join_kernel, float(seqlen), tokens),
        in_specs=[VMEM, VMEM],
        out_specs=VMEM,
        out_shape=jax.ShapeDtypeStruct((n_data, 2, LANES), F32),
        compiler_params=params,
        name="join",
    )(got, own)

    shared = exchange(shares, "dp", DP_ORDER)

    grad_input = pl.pallas_call(
        functools.partial(input_kernel, tokens),
        in_specs=[SMEM, VMEM, VMEM, VMEM],
        out_specs=HBM,
        out_shape=jax.ShapeDtypeStruct((tokens, chans), BF16),
        scratch_shapes=[
            pltpu.VMEM((tokens, LANES), F32),
            pltpu.VMEM((halves, tokens, LANES), BF16),
            pltpu.SemaphoreType.DMA((2,)),
        ],
        compiler_params=params,
        cost_estimate=pl.CostEstimate(
            flops=4 * tokens * chans * modes, bytes_accessed=4 * tokens * chans, transcendentals=0
        ),
        name="input_gradient",
    )(me, got, state, wide)

    grad_residue, grad_lograte = pl.pallas_call(
        total_kernel,
        in_specs=[VMEM],
        out_specs=[VMEM, VMEM],
        out_shape=[jax.ShapeDtypeStruct((modes, OWN), F32)] * 2,
        compiler_params=params,
        name="total",
    )(shared)
    return grad_input, grad_residue.T, grad_lograte.T


def solution(mesh):
    in_specs = (P("ctx", "dp"), P("ctx", "dp"), P(), P())
    out_specs = (P("ctx", "dp"), P("ctx", None), P("ctx", None))
    return jax.shard_map(
        on_device, mesh=mesh, in_specs=in_specs, out_specs=out_specs, check_vma=False
    )
```

```python
import functools

import jax
import jax.numpy as jnp
from jax import lax
from jax.experimental import pallas as pl
from jax.experimental.pallas import tpu as pltpu
from jax.sharding import PartitionSpec as P

LANES = 128
SUBS = 8
OWN = 16
STEP = 4
SOME = 2
CTX_ORDER = [10, 2, 3, 1, 0, 12, 13, 15, 14, 4, 5, 7, 6, 11, 9, 8]
DP_ORDER = [23, 21, 22, 24, 25, 26, 27, 28, 29, 30, 31, 0, 1, 2, 3, 4, 5, 6, 7, 8, 9, 10, 11, 12, 13, 14, 15, 16, 17, 18, 19, 20]
F32 = jnp.float32
BF16 = jnp.bfloat16
VMEM = pl.BlockSpec(memory_space=pltpu.VMEM)
HBM = pl.BlockSpec(memory_space=pltpu.HBM)


def interleave(src_ref, dst_ref, base):
    run = src_ref.shape[0] // SUBS

    @pl.loop(0, run // 16)
    def _(i):
        for c in range(SUBS):
            rows = src_ref[pl.ds(pl.multiple_of(c * run + i * 16, 16), 16), :]
            dst_ref[pl.ds(base + i * (16 * SUBS) + c, 16, stride=SUBS), :] = rows.astype(F32)


def step_of(ref, base, b):
    size = STEP * SUBS
    rows = ref[pl.ds(pl.multiple_of(base + b * size, size), size), :]
    return [rows[j * SUBS : (j + 1) * SUBS] for j in range(STEP)]


def summary_kernel(
    seqlen, g_hbm, x_hbm, lr_hbm, rs_hbm,
    send_ref, state_ref, wide_ref, own_ref,
    gb, xb, lr_ref, rs_ref, xs, acc, sems,
):
    tokens = g_hbm.shape[0]
    halves = g_hbm.shape[1] // LANES
    run = tokens // SUBS
    steps = run // STEP
    modes = lr_hbm.shape[0]

    def column(hbm, buf, half, sem):
        return pltpu.make_async_copy(hbm.at[:, pl.ds(half * LANES, LANES)], buf.at[half], sem)

    small = [
        column(hbm, buf, half, sems.at[2 * i + half])
        for i, (hbm, buf) in enumerate(((lr_hbm, lr_ref), (rs_hbm, rs_ref)))
        for half in range(halves)
    ]
    large = [
        [column(g_hbm, gb, half, sems.at[4 + half]), column(x_hbm, xb, half, sems.at[6 + half])]
        for half in range(halves)
    ]
    for copy in large[0] + small + large[1]:
        copy.start()
    for copy in small:
        copy.wait()

    def scan(half):
        base = half * tokens
        for i, (hbm, src, dst, at) in enumerate(((g_hbm, gb, wide_ref, base), (x_hbm, xb, xs, 0))):
            column(hbm, src, half, sems.at[4 + 2 * i + half]).wait()
            interleave(src.at[half], dst, at)
        rate = jnp.exp(lr_ref[half])
        zero = rate * 0.0
        for first in range(0, modes, SOME):
            rows = [jnp.broadcast_to(rate[m : m + 1], (SUBS, LANES)) for m in range(first, first + SOME)]
            decay = [jnp.exp(-r) for r in rows]
            part = [a * (1.0 / STEP) for a in decay]
            leap = [jnp.exp(-float(STEP) * r) for r in rows]

            def step(i, carry):
                b = steps - 1 - i
                g0, g1, g2, g3 = step_of(wide_ref, base, b)
                x0, x1, x2, x3 = step_of(xs, 0, b)
                out = []
                for a, a_part, a4, (w, q, r, l, n, f, p) in zip(decay, part, leap, carry):
                    y0 = a * x0
                    y1 = x1 + y0
                    y2 = x2 + a * y1
                    v = x3 + a * y2
                    dv = a_part * (y2 + a * (y1 + y0))
                    r = r + v * w
                    l = l + (v * q + dv * w)
                    n = n + p * v
                    f = f + (p * dv - n)
                    p = p * a4
                    h = a * g3
                    t2 = g2 + h
                    t1 = g1 + a * t2
                    u = g0 + a * t1
                    du = a_part * (t1 + a * (t2 + h))
                    z = a4 * w
                    q = (du + a4 * q) + z
                    w = u + z
                    out.append((w, q, r, l, n, f, p))
                if first == 0:
                    c0, c1, c2, c3 = carry[SOME]
                    out.append((
                        c0 + ((g0 * x0 + g1 * x1) + (g2 * x2 + g3 * x3)),
                        c1 + ((g1 * x0 + g2 * x1) + g3 * x2),
                        c2 + (g2 * x0 + g3 * x1),
                        c3 + g3 * x0,
                    ))
                return tuple(out)

            start = ((zero,) * 6 + (zero + 1.0,),) * SOME
            if first == 0:
                start = start + ((zero,) * 4,)
            sums = lax.fori_loop(0, steps, step, start, unroll=16)
            if first == 0:
                c0, c1, c2, c3 = sums[SOME]
            for k in range(SOME):
                w, q, r, l, n, f, _ = sums[k]
                a = decay[k]
                k1, k2, k3 = a * c1, a * a * c2, a * a * a * c3
                values = (
                    w,
                    float(STEP) * q,
                    a * r + (c0 + k1) + (k2 + k3),
                    a * (float(STEP) * l + r) + k1 + 2.0 * k2 + 3.0 * k3,
                    a * n,
                    a * (n + float(STEP) * (f + float(steps) * n)),
                )
                for j in range(6):
                    acc[half, j, (first + k) * SUBS : (first + k + 1) * SUBS, :] = values[j]

    both = range(halves)
    pl.loop(0, halves)(scan)

    def of_run(j, c):
        return [acc[half, j, pl.ds(c, modes, stride=SUBS), :] for half in both]

    def each(rule, *columns):
        return [rule(*values) for values in zip(*columns)]

    rate = [jnp.exp(lr_ref[half]) for half in both]
    leap = each(lambda r: jnp.exp(-float(run) * r), rate)
    w = q = res = lag = near = far = each(lambda r: r * 0.0, rate)
    for i in range(SUBS):
        c = SUBS - 1 - i
        wc, qc, rc, lc, nc, fc = (of_run(j, c) for j in range(6))
        for half in both:
            state_ref[half, pl.ds(c, modes, stride=SUBS), :] = w[half]
        res = each(lambda t, r, n, w: t + r + n * w, res, rc, nc, w)
        lag = each(lambda t, l, n, f, w, q: t + l + (n * q + f * w), lag, lc, nc, fc, w, q)
        z = each(lambda a, w: a * w, leap, w)
        q = each(lambda qc, a, q, z: qc + a * q + float(run) * z, qc, leap, q, z)
        w = each(lambda wc, z: wc + z, wc, z)
        nc, fc = of_run(4, i), of_run(5, i)
        z = each(lambda a, n: a * n, leap, near)
        far = each(lambda fc, a, f, z: fc + a * f + float(run) * z, fc, leap, far, z)
        near = each(lambda nc, z: nc + z, nc, z)

    slot = lax.broadcasted_iota(jnp.int32, (SUBS, LANES), 1) // OWN
    ahead = jnp.concatenate(w, axis=0)
    for half in both:
        state_ref[half, modes * SUBS : modes * SUBS + modes, :] = rate[half]
        state_ref[half, modes * SUBS + modes : modes * SUBS + 2 * modes, :] = rs_ref[half]
        res_high, lag_high = res[half].astype(BF16).astype(F32), lag[half].astype(BF16).astype(F32)
        parts = (
            w[half], q[half], near[half], far[half],
            res_high, lag_high, res[half] - res_high, lag[half] - lag_high,
        )
        for d in range(LANES // OWN):
            packed = parts[d]
            for j, part in enumerate(parts):
                if j != d:
                    packed = jnp.where(slot == j, pltpu.roll(part, ((j - d) * OWN) % LANES, 1), packed)
            place = CTX_ORDER.index(half * (LANES // OWN) + d)
            send_ref[place, :, :] = jnp.concatenate([ahead, packed], axis=0).astype(BF16)

    me = lax.axis_index("ctx")
    slots = LANES // OWN
    upper = me >= slots
    shift = jnp.where(me % slots == 0, 0, LANES - (me % slots) * OWN)
    rate = jnp.exp(pltpu.roll(jnp.where(upper, lr_ref[1], lr_ref[0]), shift, 1))
    resid = pltpu.roll(jnp.where(upper, rs_ref[1], rs_ref[0]), shift, 1)
    own_ref[0:SUBS, :] = jnp.exp(-float(tokens) * rate)
    own_ref[SUBS : 2 * SUBS, :] = -rate * resid * (1.0 / seqlen)


def join_kernel(seqlen, tokens, got_ref, own_ref, send_ref):
    blocks = got_ref.shape[0]

    def slot(tile, j):
        return pltpu.roll(tile, LANES - OWN * j, 1)

    span = own_ref[0:SUBS, :]
    w = q = res = lag = every = jnp.zeros((SUBS, LANES), F32)
    for k in range(blocks - 1, -1, -1):
        tile = got_ref[CTX_ORDER.index(k), :, :].astype(F32)[2 * SUBS : 3 * SUBS]
        every = every + tile
        near = slot(tile, 2)
        res = res + near * w
        lag = lag + near * q + slot(tile, 3) * w
        z = span * w
        q = slot(tile, 1) + span * q + float(tokens) * z
        w = tile + z
    res = (res + (slot(every, 4) + slot(every, 6))) * (1.0 / seqlen)
    lag = (lag + (slot(every, 5) + slot(every, 7))) * own_ref[SUBS : 2 * SUBS, :]
    lane = lax.broadcasted_iota(jnp.int32, (SUBS, LANES), 1)

    def in_a_row(tile):
        tile = pltpu.roll(jnp.where(lane < OWN, tile, 0.0), 0, 1, stride=OWN, stride_axis=0)
        return jnp.sum(tile, axis=0, keepdims=True)

    rows = jnp.concatenate([in_a_row(res), in_a_row(lag)], axis=0)
    send_ref[...] = jnp.broadcast_to(rows[None], send_ref.shape)


def input_kernel(tokens, got_ref, state_ref, wide_ref, out_hbm, os, ob, sems):
    run = tokens // SUBS
    steps = run // STEP
    halves = state_ref.shape[0]
    modes = SUBS
    me = lax.axis_index("ctx")
    rates = [state_ref[half, modes * SUBS : modes * SUBS + modes, :] for half in range(halves)]
    span = jnp.exp(-float(tokens) * jnp.concatenate(rates, axis=0))
    enter = jnp.zeros_like(span)
    for k in range(got_ref.shape[0] - 1, 0, -1):
        tile = got_ref[CTX_ORDER.index(k), :, :].astype(F32)[: halves * modes]
        enter = jnp.where(k > me, tile + span * enter, enter)
    after = (SUBS - 1) - lax.broadcasted_iota(jnp.int32, (SUBS, LANES), 0)
    runs_left = after.astype(F32) * float(run)

    def writeback(half):
        return pltpu.make_async_copy(ob.at[half], out_hbm.at[:, pl.ds(half * LANES, LANES)], sems.at[half])

    for half in range(halves):
        base = half * tokens
        decay, resid, start = [], [], []
        for m in range(modes):
            at = modes * SUBS + m
            rm = jnp.broadcast_to(state_ref[half, at : at + 1, :], (SUBS, LANES))
            decay.append(jnp.exp(-rm))
            resid.append(jnp.broadcast_to(state_ref[half, at + modes : at + modes + 1, :], (SUBS, LANES)))
            row = half * modes + m
            start.append(
                state_ref[half, m * SUBS : (m + 1) * SUBS, :] + jnp.exp(-rm * runs_left) * enter[row : row + 1]
            )

        def step(i, carry):
            b = steps - 1 - i
            values = step_of(wide_ref, base, b)
            sums = [None] * STEP
            for j in range(STEP - 1, -1, -1):
                carry = tuple(a * w + values[j] for a, w in zip(decay, carry))
                terms = [r * w for r, w in zip(resid, carry)]
                while len(terms) > 1:
                    terms = [a + b for a, b in zip(terms[::2], terms[1::2])]
                sums[j] = terms[0]
            size = STEP * SUBS
            os[pl.ds(pl.multiple_of(b * size, size), size), :] = jnp.concatenate(sums, axis=0)
            return carry

        lax.fori_loop(0, steps, step, tuple(start), unroll=2)

        @pl.loop(0, run // 16)
        def _(i):
            for c in range(SUBS):
                rows = os[pl.ds(i * (16 * SUBS) + c, 16, stride=SUBS), :]
                ob[half, pl.ds(pl.multiple_of(c * run + i * 16, 16), 16), :] = rows.astype(BF16)

        writeback(half).start()
    for half in range(halves):
        writeback(half).wait()


def total_kernel(got_ref, res_ref, lag_ref):
    total = got_ref[0, :, :]
    for k in range(1, got_ref.shape[0]):
        total = total + got_ref[k, :, :]
    mode = lax.broadcasted_iota(jnp.int32, (SUBS, LANES), 0)
    for j, out in enumerate((res_ref, lag_ref)):
        row = jnp.broadcast_to(total[j : j + 1], (SUBS, LANES))
        tile = row
        for m in range(1, SUBS):
            tile = jnp.where(mode == m, pltpu.roll(row, LANES - OWN * m, 1), tile)
        out[...] = tile[:, :OWN]


def exchange(blocks, axis, order):
    return lax.all_to_all(
        blocks, axis, split_axis=0, concat_axis=0, axis_index_groups=[order], tiled=True
    )


def on_device(grad_out, conv_input, residues, log_rate):
    n_context, n_data = lax.axis_size("ctx"), lax.axis_size("dp")
    tokens, chans = grad_out.shape
    modes = residues.shape[1]
    seqlen = tokens * n_context
    halves = chans // LANES
    params = pltpu.CompilerParams(vmem_limit_bytes=24 * 1024 * 1024)

    send, state, wide, own = pl.pallas_call(
        functools.partial(summary_kernel, float(seqlen)),
        in_specs=[HBM, HBM, HBM, HBM],
        out_specs=[VMEM, VMEM, VMEM, VMEM],
        out_shape=[
            jax.ShapeDtypeStruct((n_context, 3 * SUBS, LANES), BF16),
            jax.ShapeDtypeStruct((halves, modes * SUBS + 2 * modes, LANES), F32),
            jax.ShapeDtypeStruct((halves * tokens, LANES), F32),
            jax.ShapeDtypeStruct((2 * SUBS, LANES), F32),
        ],
        scratch_shapes=[
            pltpu.VMEM((halves, tokens, LANES), BF16),
            pltpu.VMEM((halves, tokens, LANES), BF16),
            pltpu.VMEM((halves, modes, LANES), F32),
            pltpu.VMEM((halves, modes, LANES), F32),
            pltpu.VMEM((tokens, LANES), F32),
            pltpu.VMEM((halves, 6, modes * SUBS, LANES), F32),
            pltpu.SemaphoreType.DMA((8,)),
        ],
        compiler_params=params,
        name="summary",
    )(*(
        pltpu.with_memory_space_constraint(array, pltpu.HBM)
        for array in (grad_out, conv_input, log_rate.T, residues.T)
    ))

    got = exchange(send, "ctx", CTX_ORDER)

    shares = pl.pallas_call(
        functools.partial(join_kernel, float(seqlen), tokens),
        in_specs=[VMEM, VMEM],
        out_specs=VMEM,
        out_shape=jax.ShapeDtypeStruct((n_data, 2, LANES), F32),
        compiler_params=params,
        name="join",
    )(got, own)

    shared = exchange(shares, "dp", DP_ORDER)

    grad_input = pl.pallas_call(
        functools.partial(input_kernel, tokens),
        in_specs=[VMEM, VMEM, VMEM],
        out_specs=HBM,
        out_shape=jax.ShapeDtypeStruct((tokens, chans), BF16),
        scratch_shapes=[
            pltpu.VMEM((tokens, LANES), F32),
            pltpu.VMEM((halves, tokens, LANES), BF16),
            pltpu.SemaphoreType.DMA((2,)),
        ],
        compiler_params=params,
        cost_estimate=pl.CostEstimate(
            flops=4 * tokens * chans * modes, bytes_accessed=4 * tokens * chans, transcendentals=0
        ),
        name="input_gradient",
    )(got, state, wide)

    grad_residue, grad_lograte = pl.pallas_call(
        total_kernel,
        in_specs=[VMEM],
        out_specs=[VMEM, VMEM],
        out_shape=[jax.ShapeDtypeStruct((modes, OWN), F32)] * 2,
        compiler_params=params,
        name="total",
    )(shared)
    return grad_input, grad_residue.T, grad_lograte.T


def solution(mesh):
    in_specs = (P("ctx", "dp"), P("ctx", "dp"), P(), P())
    out_specs = (P("ctx", "dp"), P("ctx", None), P("ctx", None))
    return jax.shard_map(
        on_device, mesh=mesh, in_specs=in_specs, out_specs=out_specs, check_vma=False
    )
```

```python
import functools

import jax
import jax.numpy as jnp
from jax import lax
from jax.experimental import pallas as pl
from jax.experimental.pallas import tpu as pltpu
from jax.sharding import PartitionSpec as P

LANES = 128
SUBS = 8
OWN = 16
STEP = 4
SOME = 2
CTX_ORDER = [10, 2, 3, 1, 0, 12, 13, 15, 14, 4, 5, 7, 6, 11, 9, 8]
DP_ORDER = [23, 21, 22, 24, 25, 26, 27, 28, 29, 30, 31, 0, 1, 2, 3, 4, 5, 6, 7, 8, 9, 10, 11, 12, 13, 14, 15, 16, 17, 18, 19, 20]
F32 = jnp.float32
BF16 = jnp.bfloat16
VMEM = pl.BlockSpec(memory_space=pltpu.VMEM)
HBM = pl.BlockSpec(memory_space=pltpu.HBM)


def interleave(src_ref, dst_ref, base):
    run = src_ref.shape[0] // SUBS

    @pl.loop(0, run // 16, unroll=8)
    def _(i):
        for c in range(SUBS):
            rows = src_ref[pl.ds(pl.multiple_of(c * run + i * 16, 16), 16), :]
            dst_ref[pl.ds(base + i * (16 * SUBS) + c, 16, stride=SUBS), :] = rows.astype(F32)


def step_of(ref, base, b):
    size = STEP * SUBS
    rows = ref[pl.ds(pl.multiple_of(base + b * size, size), size), :]
    return [rows[j * SUBS : (j + 1) * SUBS] for j in range(STEP)]


def summary_kernel(
    seqlen, g_hbm, x_hbm, lr_hbm, rs_hbm,
    send_ref, state_ref, wide_ref, own_ref,
    gb, xb, lr_ref, rs_ref, xs, acc, sems,
):
    tokens = g_hbm.shape[0]
    halves = g_hbm.shape[1] // LANES
    run = tokens // SUBS
    steps = run // STEP
    modes = lr_hbm.shape[0]

    def column(hbm, buf, half, sem):
        return pltpu.make_async_copy(hbm.at[:, pl.ds(half * LANES, LANES)], buf.at[half], sem)

    small = [
        column(hbm, buf, half, sems.at[2 * i + half])
        for i, (hbm, buf) in enumerate(((lr_hbm, lr_ref), (rs_hbm, rs_ref)))
        for half in range(halves)
    ]
    large = [
        [column(g_hbm, gb, half, sems.at[4 + half]), column(x_hbm, xb, half, sems.at[6 + half])]
        for half in range(halves)
    ]
    for copy in large[0] + small + large[1]:
        copy.start()
    for copy in small:
        copy.wait()

    me = lax.axis_index("ctx")
    slots = LANES // OWN
    upper = me >= slots
    shift = jnp.where(me % slots == 0, 0, LANES - (me % slots) * OWN)
    rate = jnp.exp(pltpu.roll(jnp.where(upper, lr_ref[1], lr_ref[0]), shift, 1))
    resid = pltpu.roll(jnp.where(upper, rs_ref[1], rs_ref[0]), shift, 1)
    own_ref[0:SUBS, :] = jnp.exp(-float(tokens) * rate)
    own_ref[SUBS : 2 * SUBS, :] = -rate * resid * (1.0 / seqlen)


    def scan(half):
        base = half * tokens
        for i, (hbm, src, dst, at) in enumerate(((g_hbm, gb, wide_ref, base), (x_hbm, xb, xs, 0))):
            column(hbm, src, half, sems.at[4 + 2 * i + half]).wait()
            interleave(src.at[half], dst, at)
        rate = jnp.exp(lr_ref[half])
        zero = rate * 0.0
        for first in range(0, modes, SOME):
            rows = [jnp.broadcast_to(rate[m : m + 1], (SUBS, LANES)) for m in range(first, first + SOME)]
            decay = [jnp.exp(-r) for r in rows]
            part = [a * (1.0 / STEP) for a in decay]
            leap = [jnp.exp(-float(STEP) * r) for r in rows]

            def step(i, carry):
                b = steps - 1 - i
                g0, g1, g2, g3 = step_of(wide_ref, base, b)
                x0, x1, x2, x3 = step_of(xs, 0, b)
                out = []
                for a, a_part, a4, (w, q, r, l, n, f, p) in zip(decay, part, leap, carry):
                    y0 = a * x0
                    y1 = x1 + y0
                    y2 = x2 + a * y1
                    v = x3 + a * y2
                    dv = a_part * (y2 + a * (y1 + y0))
                    r = r + v * w
                    l = l + (v * q + dv * w)
                    n = n + p * v
                    f = f + (p * dv - n)
                    p = p * a4
                    h = a * g3
                    t2 = g2 + h
                    t1 = g1 + a * t2
                    u = g0 + a * t1
                    du = a_part * (t1 + a * (t2 + h))
                    z = a4 * w
                    q = (du + a4 * q) + z
                    w = u + z
                    out.append((w, q, r, l, n, f, p))
                if first == 0:
                    c0, c1, c2, c3 = carry[SOME]
                    out.append((
                        c0 + ((g0 * x0 + g1 * x1) + (g2 * x2 + g3 * x3)),
                        c1 + ((g1 * x0 + g2 * x1) + g3 * x2),
                        c2 + (g2 * x0 + g3 * x1),
                        c3 + g3 * x0,
                    ))
                return tuple(out)

            start = ((zero,) * 6 + (zero + 1.0,),) * SOME
            if first == 0:
                start = start + ((zero,) * 4,)
            sums = lax.fori_loop(0, steps, step, start, unroll=16)
            if first == 0:
                c0, c1, c2, c3 = sums[SOME]
            for k in range(SOME):
                w, q, r, l, n, f, _ = sums[k]
                a = decay[k]
                k1, k2, k3 = a * c1, a * a * c2, a * a * a * c3
                values = (
                    w,
                    float(STEP) * q,
                    a * r + (c0 + k1) + (k2 + k3),
                    a * (float(STEP) * l + r) + k1 + 2.0 * k2 + 3.0 * k3,
                    a * n,
                    a * (n + float(STEP) * (f + float(steps) * n)),
                )
                for j in range(6):
                    acc[half, j, (first + k) * SUBS : (first + k + 1) * SUBS, :] = values[j]

    both = range(halves)
    pl.loop(0, halves)(scan)

    def of_run(j, c):
        return [acc[half, j, pl.ds(c, modes, stride=SUBS), :] for half in both]

    def each(rule, *columns):
        return [rule(*values) for values in zip(*columns)]

    rate = [jnp.exp(lr_ref[half]) for half in both]
    leap = each(lambda r: jnp.exp(-float(run) * r), rate)
    w = q = res = lag = near = far = each(lambda r: r * 0.0, rate)
    for i in range(SUBS):
        c = SUBS - 1 - i
        wc, qc, rc, lc, nc, fc = (of_run(j, c) for j in range(6))
        for half in both:
            state_ref[half, pl.ds(c, modes, stride=SUBS), :] = w[half]
        res = each(lambda t, r, n, w: t + r + n * w, res, rc, nc, w)
        lag = each(lambda t, l, n, f, w, q: t + l + (n * q + f * w), lag, lc, nc, fc, w, q)
        z = each(lambda a, w: a * w, leap, w)
        q = each(lambda qc, a, q, z: qc + a * q + float(run) * z, qc, leap, q, z)
        w = each(lambda wc, z: wc + z, wc, z)
        nc, fc = of_run(4, i), of_run(5, i)
        z = each(lambda a, n: a * n, leap, near)
        far = each(lambda fc, a, f, z: fc + a * f + float(run) * z, fc, leap, far, z)
        near = each(lambda nc, z: nc + z, nc, z)

    slot = lax.broadcasted_iota(jnp.int32, (SUBS, LANES), 1) // OWN
    ahead = jnp.concatenate(w, axis=0)
    for half in both:
        state_ref[half, modes * SUBS : modes * SUBS + modes, :] = rate[half]
        state_ref[half, modes * SUBS + modes : modes * SUBS + 2 * modes, :] = rs_ref[half]
        res_high, lag_high = res[half].astype(BF16).astype(F32), lag[half].astype(BF16).astype(F32)
        parts = (
            w[half], q[half], near[half], far[half],
            res_high, lag_high, res[half] - res_high, lag[half] - lag_high,
        )
        for d in range(LANES // OWN):
            packed = parts[d]
            for j, part in enumerate(parts):
                if j != d:
                    packed = jnp.where(slot == j, pltpu.roll(part, ((j - d) * OWN) % LANES, 1), packed)
            place = CTX_ORDER.index(half * (LANES // OWN) + d)
            send_ref[place, :, :] = jnp.concatenate([ahead, packed], axis=0).astype(BF16)


def join_kernel(seqlen, tokens, got_ref, own_ref, send_ref):
    blocks = got_ref.shape[0]

    def slot(tile, j):
        return pltpu.roll(tile, LANES - OWN * j, 1)

    span = own_ref[0:SUBS, :]
    w = q = res = lag = every = jnp.zeros((SUBS, LANES), F32)
    for k in range(blocks - 1, -1, -1):
        tile = got_ref[CTX_ORDER.index(k), :, :].astype(F32)[2 * SUBS : 3 * SUBS]
        every = every + tile
        near = slot(tile, 2)
        res = res + near * w
        lag = lag + near * q + slot(tile, 3) * w
        z = span * w
        q = slot(tile, 1) + span * q + float(tokens) * z
        w = tile + z
    res = (res + (slot(every, 4) + slot(every, 6))) * (1.0 / seqlen)
    lag = (lag + (slot(every, 5) + slot(every, 7))) * own_ref[SUBS : 2 * SUBS, :]
    lane = lax.broadcasted_iota(jnp.int32, (SUBS, LANES), 1)

    def in_a_row(tile):
        tile = pltpu.roll(jnp.where(lane < OWN, tile, 0.0), 0, 1, stride=OWN, stride_axis=0)
        return jnp.sum(tile, axis=0, keepdims=True)

    rows = jnp.concatenate([in_a_row(res), in_a_row(lag)], axis=0)
    send_ref[...] = jnp.broadcast_to(rows[None], send_ref.shape)


def input_kernel(tokens, got_ref, state_ref, wide_ref, out_hbm, os, ob, sems):
    run = tokens // SUBS
    steps = run // STEP
    halves = state_ref.shape[0]
    modes = SUBS
    me = lax.axis_index("ctx")
    rates = [state_ref[half, modes * SUBS : modes * SUBS + modes, :] for half in range(halves)]
    span = jnp.exp(-float(tokens) * jnp.concatenate(rates, axis=0))
    enter = jnp.zeros_like(span)
    for k in range(got_ref.shape[0] - 1, 0, -1):
        tile = got_ref[CTX_ORDER.index(k), :, :].astype(F32)[: halves * modes]
        enter = jnp.where(k > me, tile + span * enter, enter)
    after = (SUBS - 1) - lax.broadcasted_iota(jnp.int32, (SUBS, LANES), 0)
    runs_left = after.astype(F32) * float(run)

    def writeback(half):
        return pltpu.make_async_copy(ob.at[half], out_hbm.at[:, pl.ds(half * LANES, LANES)], sems.at[half])

    for half in range(halves):
        base = half * tokens
        decay, resid, start = [], [], []
        for m in range(modes):
            at = modes * SUBS + m
            rm = jnp.broadcast_to(state_ref[half, at : at + 1, :], (SUBS, LANES))
            decay.append(jnp.exp(-rm))
            resid.append(jnp.broadcast_to(state_ref[half, at + modes : at + modes + 1, :], (SUBS, LANES)))
            row = half * modes + m
            start.append(
                state_ref[half, m * SUBS : (m + 1) * SUBS, :] + jnp.exp(-rm * runs_left) * enter[row : row + 1]
            )

        def step(i, carry):
            b = steps - 1 - i
            values = step_of(wide_ref, base, b)
            sums = [None] * STEP
            for j in range(STEP - 1, -1, -1):
                carry = tuple(a * w + values[j] for a, w in zip(decay, carry))
                terms = [r * w for r, w in zip(resid, carry)]
                while len(terms) > 1:
                    terms = [a + b for a, b in zip(terms[::2], terms[1::2])]
                sums[j] = terms[0]
            size = STEP * SUBS
            os[pl.ds(pl.multiple_of(b * size, size), size), :] = jnp.concatenate(sums, axis=0)
            return carry

        lax.fori_loop(0, steps, step, tuple(start), unroll=4)

        @pl.loop(0, run // 16, unroll=8)
        def _(i):
            for c in range(SUBS):
                rows = os[pl.ds(i * (16 * SUBS) + c, 16, stride=SUBS), :]
                ob[half, pl.ds(pl.multiple_of(c * run + i * 16, 16), 16), :] = rows.astype(BF16)

        writeback(half).start()
    for half in range(halves):
        writeback(half).wait()


def total_kernel(got_ref, res_ref, lag_ref):
    total = got_ref[0, :, :]
    for k in range(1, got_ref.shape[0]):
        total = total + got_ref[k, :, :]
    mode = lax.broadcasted_iota(jnp.int32, (SUBS, LANES), 0)
    for j, out in enumerate((res_ref, lag_ref)):
        row = jnp.broadcast_to(total[j : j + 1], (SUBS, LANES))
        tile = row
        for m in range(1, SUBS):
            tile = jnp.where(mode == m, pltpu.roll(row, LANES - OWN * m, 1), tile)
        out[...] = tile[:, :OWN]


def exchange(blocks, axis, order):
    return lax.all_to_all(
        blocks, axis, split_axis=0, concat_axis=0, axis_index_groups=[order], tiled=True
    )


def on_device(grad_out, conv_input, residues, log_rate):
    n_context, n_data = lax.axis_size("ctx"), lax.axis_size("dp")
    tokens, chans = grad_out.shape
    modes = residues.shape[1]
    seqlen = tokens * n_context
    halves = chans // LANES
    params = pltpu.CompilerParams(vmem_limit_bytes=24 * 1024 * 1024)

    send, state, wide, own = pl.pallas_call(
        functools.partial(summary_kernel, float(seqlen)),
        in_specs=[HBM, HBM, HBM, HBM],
        out_specs=[VMEM, VMEM, VMEM, VMEM],
        out_shape=[
            jax.ShapeDtypeStruct((n_context, 3 * SUBS, LANES), BF16),
            jax.ShapeDtypeStruct((halves, modes * SUBS + 2 * modes, LANES), F32),
            jax.ShapeDtypeStruct((halves * tokens, LANES), F32),
            jax.ShapeDtypeStruct((2 * SUBS, LANES), F32),
        ],
        scratch_shapes=[
            pltpu.VMEM((halves, tokens, LANES), BF16),
            pltpu.VMEM((halves, tokens, LANES), BF16),
            pltpu.VMEM((halves, modes, LANES), F32),
            pltpu.VMEM((halves, modes, LANES), F32),
            pltpu.VMEM((tokens, LANES), F32),
            pltpu.VMEM((halves, 6, modes * SUBS, LANES), F32),
            pltpu.SemaphoreType.DMA((8,)),
        ],
        compiler_params=params,
        name="summary",
    )(*(
        pltpu.with_memory_space_constraint(array, pltpu.HBM)
        for array in (grad_out, conv_input, log_rate.T, residues.T)
    ))

    got = exchange(send, "ctx", CTX_ORDER)

    shares = pl.pallas_call(
        functools.partial(join_kernel, float(seqlen), tokens),
        in_specs=[VMEM, VMEM],
        out_specs=VMEM,
        out_shape=jax.ShapeDtypeStruct((n_data, 2, LANES), F32),
        compiler_params=params,
        name="join",
    )(got, own)

    shared = exchange(shares, "dp", DP_ORDER)

    grad_input = pl.pallas_call(
        functools.partial(input_kernel, tokens),
        in_specs=[VMEM, VMEM, VMEM],
        out_specs=HBM,
        out_shape=jax.ShapeDtypeStruct((tokens, chans), BF16),
        scratch_shapes=[
            pltpu.VMEM((tokens, LANES), F32),
            pltpu.VMEM((halves, tokens, LANES), BF16),
            pltpu.SemaphoreType.DMA((2,)),
        ],
        compiler_params=params,
        cost_estimate=pl.CostEstimate(
            flops=4 * tokens * chans * modes, bytes_accessed=4 * tokens * chans, transcendentals=0
        ),
        name="input_gradient",
    )(got, state, wide)

    grad_residue, grad_lograte = pl.pallas_call(
        total_kernel,
        in_specs=[VMEM],
        out_specs=[VMEM, VMEM],
        out_shape=[jax.ShapeDtypeStruct((modes, OWN), F32)] * 2,
        compiler_params=params,
        name="total",
    )(shared)
    return grad_input, grad_residue.T, grad_lograte.T


def solution(mesh):
    in_specs = (P("ctx", "dp"), P("ctx", "dp"), P(), P())
    out_specs = (P("ctx", "dp"), P("ctx", None), P("ctx", None))
    return jax.shard_map(
        on_device, mesh=mesh, in_specs=in_specs, out_specs=out_specs, check_vma=False
    )
```

```python
import functools

import jax
import jax.numpy as jnp
from jax import lax
from jax.experimental import pallas as pl
from jax.experimental.pallas import tpu as pltpu
from jax.sharding import PartitionSpec as P

LANES = 128
SUBS = 8
OWN = 16
STEP = 4
SOME = 2
CTX_ORDER = [10, 2, 3, 1, 0, 12, 13, 15, 14, 4, 5, 7, 6, 11, 9, 8]
DP_ORDER = [23, 21, 22, 24, 25, 26, 27, 28, 29, 30, 31, 0, 1, 2, 3, 4, 5, 6, 7, 8, 9, 10, 11, 12, 13, 14, 15, 16, 17, 18, 19, 20]
F32 = jnp.float32
BF16 = jnp.bfloat16
VMEM = pl.BlockSpec(memory_space=pltpu.VMEM)
HBM = pl.BlockSpec(memory_space=pltpu.HBM)


def interleave(src_ref, dst_ref, base):
    run = src_ref.shape[0] // SUBS

    @pl.loop(0, run // 16, unroll=8)
    def _(i):
        for c in range(SUBS):
            rows = src_ref[pl.ds(pl.multiple_of(c * run + i * 16, 16), 16), :]
            dst_ref[pl.ds(base + i * (16 * SUBS) + c, 16, stride=SUBS), :] = rows.astype(F32)


def step_of(ref, base, b):
    size = STEP * SUBS
    rows = ref[pl.ds(pl.multiple_of(base + b * size, size), size), :]
    return [rows[j * SUBS : (j + 1) * SUBS] for j in range(STEP)]


def summary_kernel(
    seqlen, g_hbm, x_hbm, lr_hbm, rs_hbm,
    send_ref, state_ref, wide_ref, own_ref,
    gb, xb, lr_ref, rs_ref, xs, acc, sems,
):
    tokens = g_hbm.shape[0]
    halves = g_hbm.shape[1] // LANES
    run = tokens // SUBS
    steps = run // STEP
    modes = lr_hbm.shape[0]

    def column(hbm, buf, half, sem):
        return pltpu.make_async_copy(hbm.at[:, pl.ds(half * LANES, LANES)], buf.at[half], sem)

    small = [
        column(hbm, buf, half, sems.at[2 * i + half])
        for i, (hbm, buf) in enumerate(((lr_hbm, lr_ref), (rs_hbm, rs_ref)))
        for half in range(halves)
    ]
    large = [
        [column(g_hbm, gb, half, sems.at[4 + half]), column(x_hbm, xb, half, sems.at[6 + half])]
        for half in range(halves)
    ]
    for copy in large[0] + small + large[1]:
        copy.start()
    for copy in small:
        copy.wait()

    me = lax.axis_index("ctx")
    slots = LANES // OWN
    upper = me >= slots
    shift = jnp.where(me % slots == 0, 0, LANES - (me % slots) * OWN)
    rate = jnp.exp(pltpu.roll(jnp.where(upper, lr_ref[1], lr_ref[0]), shift, 1))
    resid = pltpu.roll(jnp.where(upper, rs_ref[1], rs_ref[0]), shift, 1)
    own_ref[0:SUBS, :] = jnp.exp(-float(tokens) * rate)
    own_ref[SUBS : 2 * SUBS, :] = -rate * resid * (1.0 / seqlen)


    def scan(half):
        base = half * tokens
        for i, (hbm, src, dst, at) in enumerate(((g_hbm, gb, wide_ref, base), (x_hbm, xb, xs, 0))):
            column(hbm, src, half, sems.at[4 + 2 * i + half]).wait()
            interleave(src.at[half], dst, at)
        rate = jnp.exp(lr_ref[half])
        zero = rate * 0.0
        for first in range(0, modes, SOME):
            rows = [jnp.broadcast_to(rate[m : m + 1], (SUBS, LANES)) for m in range(first, first + SOME)]
            decay = [jnp.exp(-r) for r in rows]
            part = [a * (1.0 / STEP) for a in decay]
            leap = [jnp.exp(-float(STEP) * r) for r in rows]

            def step(i, carry):
                b = steps - 1 - i
                g0, g1, g2, g3 = step_of(wide_ref, base, b)
                x0, x1, x2, x3 = step_of(xs, 0, b)
                out = []
                for a, a_part, a4, (w, q, r, l, n, f, p) in zip(decay, part, leap, carry):
                    y0 = a * x0
                    y1 = x1 + y0
                    y2 = x2 + a * y1
                    v = x3 + a * y2
                    dv = a_part * (y2 + a * (y1 + y0))
                    r = r + v * w
                    l = l + (v * q + dv * w)
                    n = n + p * v
                    f = f + (p * dv - n)
                    p = p * a4
                    h = a * g3
                    t2 = g2 + h
                    t1 = g1 + a * t2
                    u = g0 + a * t1
                    du = a_part * (t1 + a * (t2 + h))
                    z = a4 * w
                    q = (du + a4 * q) + z
                    w = u + z
                    out.append((w, q, r, l, n, f, p))
                if first == 0:
                    c0, c1, c2, c3 = carry[SOME]
                    out.append((
                        c0 + ((g0 * x0 + g1 * x1) + (g2 * x2 + g3 * x3)),
                        c1 + ((g1 * x0 + g2 * x1) + g3 * x2),
                        c2 + (g2 * x0 + g3 * x1),
                        c3 + g3 * x0,
                    ))
                return tuple(out)

            start = ((zero,) * 6 + (zero + 1.0,),) * SOME
            if first == 0:
                start = start + ((zero,) * 4,)
            sums = lax.fori_loop(0, steps, step, start, unroll=16)
            if first == 0:
                c0, c1, c2, c3 = sums[SOME]
            for k in range(SOME):
                w, q, r, l, n, f, _ = sums[k]
                a = decay[k]
                k1, k2, k3 = a * c1, a * a * c2, a * a * a * c3
                values = (
                    w,
                    float(STEP) * q,
                    a * r + (c0 + k1) + (k2 + k3),
                    a * (float(STEP) * l + r) + k1 + 2.0 * k2 + 3.0 * k3,
                    a * n,
                    a * (n + float(STEP) * (f + float(steps) * n)),
                )
                for j in range(6):
                    acc[half, j, (first + k) * SUBS : (first + k + 1) * SUBS, :] = values[j]

    both = range(halves)
    pl.loop(0, halves)(scan)

    def of_run(j, c):
        return [acc[half, j, pl.ds(c, modes, stride=SUBS), :] for half in both]

    def each(rule, *columns):
        return [rule(*values) for values in zip(*columns)]

    rate = [jnp.exp(lr_ref[half]) for half in both]
    leap = each(lambda r: jnp.exp(-float(run) * r), rate)
    w = q = res = lag = near = far = each(lambda r: r * 0.0, rate)
    for i in range(SUBS):
        c = SUBS - 1 - i
        wc, qc, rc, lc, nc, fc = (of_run(j, c) for j in range(6))
        for half in both:
            state_ref[half, pl.ds(c, modes, stride=SUBS), :] = w[half]
        res = each(lambda t, r, n, w: t + r + n * w, res, rc, nc, w)
        lag = each(lambda t, l, n, f, w, q: t + l + (n * q + f * w), lag, lc, nc, fc, w, q)
        z = each(lambda a, w: a * w, leap, w)
        q = each(lambda qc, a, q, z: qc + a * q + float(run) * z, qc, leap, q, z)
        w = each(lambda wc, z: wc + z, wc, z)
        nc, fc = of_run(4, i), of_run(5, i)
        z = each(lambda a, n: a * n, leap, near)
        far = each(lambda fc, a, f, z: fc + a * f + float(run) * z, fc, leap, far, z)
        near = each(lambda nc, z: nc + z, nc, z)

    slot = lax.broadcasted_iota(jnp.int32, (SUBS, LANES), 1) // OWN
    ahead = jnp.concatenate(w, axis=0)
    for half in both:
        state_ref[half, modes * SUBS : modes * SUBS + modes, :] = rate[half]
        state_ref[half, modes * SUBS + modes : modes * SUBS + 2 * modes, :] = rs_ref[half]
        res_high, lag_high = res[half].astype(BF16).astype(F32), lag[half].astype(BF16).astype(F32)
        parts = (
            w[half], q[half], near[half], far[half],
            res_high, lag_high, res[half] - res_high, lag[half] - lag_high,
        )
        for d in range(LANES // OWN):
            packed = parts[d]
            for j, part in enumerate(parts):
                if j != d:
                    packed = jnp.where(slot == j, pltpu.roll(part, ((j - d) * OWN) % LANES, 1), packed)
            place = CTX_ORDER.index(half * (LANES // OWN) + d)
            send_ref[place, :, :] = jnp.concatenate([ahead, packed], axis=0).astype(BF16)


def add_up(terms):
    while len(terms) > 1:
        terms = [a + b for a, b in zip(terms[::2], terms[1::2])] + terms[len(terms) & ~1 :]
    return terms[0]


def join_kernel(seqlen, tokens, got_ref, own_ref, send_ref):
    blocks = got_ref.shape[0]

    def slot(tile, j):
        return pltpu.roll(tile, LANES - OWN * j, 1)

    span = own_ref[0:SUBS, :]
    w = q = jnp.zeros((SUBS, LANES), F32)
    tiles, res, lag = [], [], []
    for k in range(blocks - 1, -1, -1):
        tile = got_ref[CTX_ORDER.index(k), :, :].astype(F32)[2 * SUBS : 3 * SUBS]
        near = slot(tile, 2)
        tiles.append(tile)
        res.append(near * w)
        lag.append(near * q + slot(tile, 3) * w)
        z = span * w
        q = (slot(tile, 1) + float(tokens) * z) + span * q
        w = tile + z
    every, res, lag = add_up(tiles), add_up(res), add_up(lag)
    res = (res + (slot(every, 4) + slot(every, 6))) * (1.0 / seqlen)
    lag = (lag + (slot(every, 5) + slot(every, 7))) * own_ref[SUBS : 2 * SUBS, :]
    lane = lax.broadcasted_iota(jnp.int32, (SUBS, LANES), 1)

    def in_a_row(tile):
        tile = pltpu.roll(jnp.where(lane < OWN, tile, 0.0), 0, 1, stride=OWN, stride_axis=0)
        return jnp.sum(tile, axis=0, keepdims=True)

    rows = jnp.concatenate([in_a_row(res), in_a_row(lag)], axis=0)
    send_ref[...] = jnp.broadcast_to(rows[None], send_ref.shape)


def input_kernel(tokens, got_ref, state_ref, wide_ref, out_hbm, os, ob, sems):
    run = tokens // SUBS
    steps = run // STEP
    halves = state_ref.shape[0]
    modes = SUBS
    me = lax.axis_index("ctx")
    rates = [state_ref[half, modes * SUBS : modes * SUBS + modes, :] for half in range(halves)]
    span = jnp.exp(-float(tokens) * jnp.concatenate(rates, axis=0))
    enter = jnp.zeros_like(span)
    for k in range(got_ref.shape[0] - 1, 0, -1):
        tile = got_ref[CTX_ORDER.index(k), :, :].astype(F32)[: halves * modes]
        enter = jnp.where(k > me, tile + span * enter, enter)
    after = (SUBS - 1) - lax.broadcasted_iota(jnp.int32, (SUBS, LANES), 0)
    runs_left = after.astype(F32) * float(run)

    def writeback(half):
        return pltpu.make_async_copy(ob.at[half], out_hbm.at[:, pl.ds(half * LANES, LANES)], sems.at[half])

    for half in range(halves):
        base = half * tokens
        decay, resid, start = [], [], []
        for m in range(modes):
            at = modes * SUBS + m
            rm = jnp.broadcast_to(state_ref[half, at : at + 1, :], (SUBS, LANES))
            decay.append(jnp.exp(-rm))
            resid.append(jnp.broadcast_to(state_ref[half, at + modes : at + modes + 1, :], (SUBS, LANES)))
            row = half * modes + m
            start.append(
                state_ref[half, m * SUBS : (m + 1) * SUBS, :] + jnp.exp(-rm * runs_left) * enter[row : row + 1]
            )

        def step(i, carry):
            b = steps - 1 - i
            values = step_of(wide_ref, base, b)
            sums = [None] * STEP
            for j in range(STEP - 1, -1, -1):
                carry = tuple(a * w + values[j] for a, w in zip(decay, carry))
                terms = [r * w for r, w in zip(resid, carry)]
                sums[j] = add_up(terms)
            size = STEP * SUBS
            os[pl.ds(pl.multiple_of(b * size, size), size), :] = jnp.concatenate(sums, axis=0)
            return carry

        lax.fori_loop(0, steps, step, tuple(start), unroll=4)

        @pl.loop(0, run // 16, unroll=8)
        def _(i):
            for c in range(SUBS):
                rows = os[pl.ds(i * (16 * SUBS) + c, 16, stride=SUBS), :]
                ob[half, pl.ds(pl.multiple_of(c * run + i * 16, 16), 16), :] = rows.astype(BF16)

        writeback(half).start()
    for half in range(halves):
        writeback(half).wait()


def total_kernel(got_ref, res_ref, lag_ref):
    total = add_up([got_ref[k, :, :] for k in range(got_ref.shape[0])])
    mode = lax.broadcasted_iota(jnp.int32, (SUBS, LANES), 0)
    for j, out in enumerate((res_ref, lag_ref)):
        row = jnp.broadcast_to(total[j : j + 1], (SUBS, LANES))
        tile = row
        for m in range(1, SUBS):
            tile = jnp.where(mode == m, pltpu.roll(row, LANES - OWN * m, 1), tile)
        out[...] = tile[:, :OWN]


def exchange(blocks, axis, order):
    return lax.all_to_all(
        blocks, axis, split_axis=0, concat_axis=0, axis_index_groups=[order], tiled=True
    )


def on_device(grad_out, conv_input, residues, log_rate):
    n_context, n_data = lax.axis_size("ctx"), lax.axis_size("dp")
    tokens, chans = grad_out.shape
    modes = residues.shape[1]
    seqlen = tokens * n_context
    halves = chans // LANES
    params = pltpu.CompilerParams(vmem_limit_bytes=24 * 1024 * 1024)

    send, state, wide, own = pl.pallas_call(
        functools.partial(summary_kernel, float(seqlen)),
        in_specs=[HBM, HBM, HBM, HBM],
        out_specs=[VMEM, VMEM, VMEM, VMEM],
        out_shape=[
            jax.ShapeDtypeStruct((n_context, 3 * SUBS, LANES), BF16),
            jax.ShapeDtypeStruct((halves, modes * SUBS + 2 * modes, LANES), F32),
            jax.ShapeDtypeStruct((halves * tokens, LANES), F32),
            jax.ShapeDtypeStruct((2 * SUBS, LANES), F32),
        ],
        scratch_shapes=[
            pltpu.VMEM((halves, tokens, LANES), BF16),
            pltpu.VMEM((halves, tokens, LANES), BF16),
            pltpu.VMEM((halves, modes, LANES), F32),
            pltpu.VMEM((halves, modes, LANES), F32),
            pltpu.VMEM((tokens, LANES), F32),
            pltpu.VMEM((halves, 6, modes * SUBS, LANES), F32),
            pltpu.SemaphoreType.DMA((8,)),
        ],
        compiler_params=params,
        name="summary",
    )(*(
        pltpu.with_memory_space_constraint(array, pltpu.HBM)
        for array in (grad_out, conv_input, log_rate.T, residues.T)
    ))

    got = exchange(send, "ctx", CTX_ORDER)

    shares = pl.pallas_call(
        functools.partial(join_kernel, float(seqlen), tokens),
        in_specs=[VMEM, VMEM],
        out_specs=VMEM,
        out_shape=jax.ShapeDtypeStruct((n_data, 2, LANES), F32),
        compiler_params=params,
        name="join",
    )(got, own)

    shared = exchange(shares, "dp", DP_ORDER)

    grad_input = pl.pallas_call(
        functools.partial(input_kernel, tokens),
        in_specs=[VMEM, VMEM, VMEM],
        out_specs=HBM,
        out_shape=jax.ShapeDtypeStruct((tokens, chans), BF16),
        scratch_shapes=[
            pltpu.VMEM((tokens, LANES), F32),
            pltpu.VMEM((halves, tokens, LANES), BF16),
            pltpu.SemaphoreType.DMA((2,)),
        ],
        compiler_params=params,
        cost_estimate=pl.CostEstimate(
            flops=4 * tokens * chans * modes, bytes_accessed=4 * tokens * chans, transcendentals=0
        ),
        name="input_gradient",
    )(got, state, wide)

    grad_residue, grad_lograte = pl.pallas_call(
        total_kernel,
        in_specs=[VMEM],
        out_specs=[VMEM, VMEM],
        out_shape=[jax.ShapeDtypeStruct((modes, OWN), F32)] * 2,
        compiler_params=params,
        name="total",
    )(shared)
    return grad_input, grad_residue.T, grad_lograte.T


def solution(mesh):
    in_specs = (P("ctx", "dp"), P("ctx", "dp"), P(), P())
    out_specs = (P("ctx", "dp"), P("ctx", None), P("ctx", None))
    return jax.shard_map(
        on_device, mesh=mesh, in_specs=in_specs, out_specs=out_specs, check_vma=False
    )
```

```python
import functools

import jax
import jax.numpy as jnp
from jax import lax
from jax.experimental import pallas as pl
from jax.experimental.pallas import tpu as pltpu
from jax.sharding import PartitionSpec as P

LANES = 128
SUBS = 8
OWN = 16
STEP = 4
SOME = 2
CTX_ORDER = [10, 2, 3, 1, 0, 12, 13, 15, 14, 4, 5, 7, 6, 11, 9, 8]
DP_ORDER = [23, 21, 22, 24, 25, 26, 27, 28, 29, 30, 31, 0, 1, 2, 3, 4, 5, 6, 7, 8, 9, 10, 11, 12, 13, 14, 15, 16, 17, 18, 19, 20]
F32 = jnp.float32
BF16 = jnp.bfloat16
VMEM = pl.BlockSpec(memory_space=pltpu.VMEM)
HBM = pl.BlockSpec(memory_space=pltpu.HBM)


def interleave(src_ref, dst_ref, base):
    run = src_ref.shape[0] // SUBS

    @pl.loop(0, run // 16, unroll=8)
    def _(i):
        for c in range(SUBS):
            rows = src_ref[pl.ds(pl.multiple_of(c * run + i * 16, 16), 16), :]
            dst_ref[pl.ds(base + i * (16 * SUBS) + c, 16, stride=SUBS), :] = rows.astype(F32)


def step_of(ref, base, b):
    size = STEP * SUBS
    rows = ref[pl.ds(pl.multiple_of(base + b * size, size), size), :]
    return [rows[j * SUBS : (j + 1) * SUBS] for j in range(STEP)]


def summary_kernel(
    seqlen, g_hbm, x_hbm, lr_hbm, rs_hbm,
    send_ref, state_ref, wide_ref, own_ref,
    gb, xb, lr_ref, rs_ref, xs, acc, sems,
):
    tokens = g_hbm.shape[0]
    halves = g_hbm.shape[1] // LANES
    run = tokens // SUBS
    steps = run // STEP
    modes = lr_hbm.shape[0]

    def column(hbm, buf, half, sem):
        return pltpu.make_async_copy(hbm.at[:, pl.ds(half * LANES, LANES)], buf.at[half], sem)

    small = [
        column(hbm, buf, half, sems.at[2 * i + half])
        for i, (hbm, buf) in enumerate(((lr_hbm, lr_ref), (rs_hbm, rs_ref)))
        for half in range(halves)
    ]
    large = [
        [column(g_hbm, gb, half, sems.at[4 + half]), column(x_hbm, xb, half, sems.at[6 + half])]
        for half in range(halves)
    ]
    for copy in large[0] + small + large[1]:
        copy.start()
    for copy in small:
        copy.wait()

    me = lax.axis_index("ctx")
    slots = LANES // OWN
    upper = me >= slots
    shift = jnp.where(me % slots == 0, 0, LANES - (me % slots) * OWN)
    rate = jnp.exp(pltpu.roll(jnp.where(upper, lr_ref[1], lr_ref[0]), shift, 1))
    resid = pltpu.roll(jnp.where(upper, rs_ref[1], rs_ref[0]), shift, 1)
    own_ref[0:SUBS, :] = jnp.exp(-float(tokens) * rate)
    own_ref[SUBS : 2 * SUBS, :] = -rate * resid * (1.0 / seqlen)


    def scan(half):
        base = half * tokens
        for i, (hbm, src, dst, at) in enumerate(((g_hbm, gb, wide_ref, base), (x_hbm, xb, xs, 0))):
            column(hbm, src, half, sems.at[4 + 2 * i + half]).wait()
            interleave(src.at[half], dst, at)
        rate = jnp.exp(lr_ref[half])
        zero = rate * 0.0
        once, four = jnp.exp(-rate), jnp.exp(-float(STEP) * rate)
        for first in range(0, modes, SOME):
            group = range(first, first + SOME)
            decay = [jnp.broadcast_to(once[m : m + 1], (SUBS, LANES)) for m in group]
            part = [a * (1.0 / STEP) for a in decay]
            leap = [jnp.broadcast_to(four[m : m + 1], (SUBS, LANES)) for m in group]

            def step(i, carry):
                b = steps - 1 - i
                g0, g1, g2, g3 = step_of(wide_ref, base, b)
                x0, x1, x2, x3 = step_of(xs, 0, b)
                out = []
                for a, a_part, a4, (w, q, r, l, n, f, p) in zip(decay, part, leap, carry):
                    y0 = a * x0
                    y1 = x1 + y0
                    y2 = x2 + a * y1
                    v = x3 + a * y2
                    dv = a_part * (y2 + a * (y1 + y0))
                    r = r + v * w
                    l = l + (v * q + dv * w)
                    n = n + p * v
                    f = f + (p * dv - n)
                    p = p * a4
                    h = a * g3
                    t2 = g2 + h
                    t1 = g1 + a * t2
                    u = g0 + a * t1
                    du = a_part * (t1 + a * (t2 + h))
                    z = a4 * w
                    q = (du + a4 * q) + z
                    w = u + z
                    out.append((w, q, r, l, n, f, p))
                if first == 0:
                    c0, c1, c2, c3 = carry[SOME]
                    out.append((
                        c0 + ((g0 * x0 + g1 * x1) + (g2 * x2 + g3 * x3)),
                        c1 + ((g1 * x0 + g2 * x1) + g3 * x2),
                        c2 + (g2 * x0 + g3 * x1),
                        c3 + g3 * x0,
                    ))
                return tuple(out)

            start = ((zero,) * 6 + (zero + 1.0,),) * SOME
            if first == 0:
                start = start + ((zero,) * 4,)
            sums = lax.fori_loop(0, steps, step, start, unroll=16)
            if first == 0:
                c0, c1, c2, c3 = sums[SOME]
            for k in range(SOME):
                w, q, r, l, n, f, _ = sums[k]
                a = decay[k]
                k1, k2, k3 = a * c1, a * a * c2, a * a * a * c3
                values = (
                    w,
                    float(STEP) * q,
                    a * r + (c0 + k1) + (k2 + k3),
                    a * (float(STEP) * l + r) + k1 + 2.0 * k2 + 3.0 * k3,
                    a * n,
                    a * (n + float(STEP) * (f + float(steps) * n)),
                )
                for j in range(6):
                    acc[half, j, (first + k) * SUBS : (first + k + 1) * SUBS, :] = values[j]

    both = range(halves)
    pl.loop(0, halves)(scan)

    def of_run(j, c):
        return [acc[half, j, pl.ds(c, modes, stride=SUBS), :] for half in both]

    def each(rule, *columns):
        return [rule(*values) for values in zip(*columns)]

    rate = [jnp.exp(lr_ref[half]) for half in both]
    leap = each(lambda r: jnp.exp(-float(run) * r), rate)
    w = q = res = lag = near = far = each(lambda r: r * 0.0, rate)
    for i in range(SUBS):
        c = SUBS - 1 - i
        wc, qc, rc, lc, nc, fc = (of_run(j, c) for j in range(6))
        for half in both:
            state_ref[half, pl.ds(c, modes, stride=SUBS), :] = w[half]
        res = each(lambda t, r, n, w: t + r + n * w, res, rc, nc, w)
        lag = each(lambda t, l, n, f, w, q: t + l + (n * q + f * w), lag, lc, nc, fc, w, q)
        z = each(lambda a, w: a * w, leap, w)
        q = each(lambda qc, a, q, z: qc + a * q + float(run) * z, qc, leap, q, z)
        w = each(lambda wc, z: wc + z, wc, z)
        nc, fc = of_run(4, i), of_run(5, i)
        z = each(lambda a, n: a * n, leap, near)
        far = each(lambda fc, a, f, z: fc + a * f + float(run) * z, fc, leap, far, z)
        near = each(lambda nc, z: nc + z, nc, z)

    slot = lax.broadcasted_iota(jnp.int32, (SUBS, LANES), 1) // OWN
    ahead = jnp.concatenate(w, axis=0)
    for half in both:
        state_ref[half, modes * SUBS : modes * SUBS + modes, :] = rate[half]
        state_ref[half, modes * SUBS + modes : modes * SUBS + 2 * modes, :] = rs_ref[half]
        res_high, lag_high = res[half].astype(BF16).astype(F32), lag[half].astype(BF16).astype(F32)
        parts = (
            w[half], q[half], near[half], far[half],
            res_high, lag_high, res[half] - res_high, lag[half] - lag_high,
        )
        slots = LANES // OWN
        turned = []
        for r in range(slots):
            mixed = parts[r]
            for p in range(1, slots):
                mixed = jnp.where(slot == p, parts[(p + r) % slots], mixed)
            turned.append(pltpu.roll(mixed, r * OWN, 1) if r else mixed)
        for d in range(slots):
            packed = turned[-d % slots]
            for j in range(1, slots):
                packed = jnp.where(slot == j, turned[(j - d) % slots], packed)
            place = CTX_ORDER.index(half * (LANES // OWN) + d)
            send_ref[place, :, :] = jnp.concatenate([ahead, packed], axis=0).astype(BF16)


def add_up(terms):
    while len(terms) > 1:
        terms = [a + b for a, b in zip(terms[::2], terms[1::2])] + terms[len(terms) & ~1 :]
    return terms[0]


def join_kernel(seqlen, tokens, got_ref, own_ref, send_ref):
    blocks = got_ref.shape[0]

    def slot(tile, j):
        return pltpu.roll(tile, LANES - OWN * j, 1)

    span = own_ref[0:SUBS, :]
    w = q = jnp.zeros((SUBS, LANES), F32)
    tiles, res, lag = [], [], []
    for k in range(blocks - 1, -1, -1):
        tile = got_ref[CTX_ORDER.index(k), :, :].astype(F32)[2 * SUBS : 3 * SUBS]
        near = slot(tile, 2)
        tiles.append(tile)
        res.append(near * w)
        lag.append(near * q + slot(tile, 3) * w)
        z = span * w
        q = (slot(tile, 1) + float(tokens) * z) + span * q
        w = tile + z
    every, res, lag = add_up(tiles), add_up(res), add_up(lag)
    res = (res + (slot(every, 4) + slot(every, 6))) * (1.0 / seqlen)
    lag = (lag + (slot(every, 5) + slot(every, 7))) * own_ref[SUBS : 2 * SUBS, :]
    lane = lax.broadcasted_iota(jnp.int32, (SUBS, LANES), 1)

    def in_a_row(tile):
        tile = pltpu.roll(jnp.where(lane < OWN, tile, 0.0), 0, 1, stride=OWN, stride_axis=0)
        return jnp.sum(tile, axis=0, keepdims=True)

    rows = jnp.concatenate([in_a_row(res), in_a_row(lag)], axis=0)
    send_ref[...] = jnp.broadcast_to(rows[None], send_ref.shape)


def input_kernel(tokens, got_ref, state_ref, wide_ref, out_hbm, os, ob, sems):
    run = tokens // SUBS
    steps = run // STEP
    halves = state_ref.shape[0]
    modes = SUBS
    me = lax.axis_index("ctx")
    rates = [state_ref[half, modes * SUBS : modes * SUBS + modes, :] for half in range(halves)]
    span = jnp.exp(-float(tokens) * jnp.concatenate(rates, axis=0))
    enter = jnp.zeros_like(span)
    for k in range(got_ref.shape[0] - 1, 0, -1):
        tile = got_ref[CTX_ORDER.index(k), :, :].astype(F32)[: halves * modes]
        enter = jnp.where(k > me, tile + span * enter, enter)
    after = (SUBS - 1) - lax.broadcasted_iota(jnp.int32, (SUBS, LANES), 0)
    runs_left = after.astype(F32) * float(run)

    def writeback(half):
        return pltpu.make_async_copy(ob.at[half], out_hbm.at[:, pl.ds(half * LANES, LANES)], sems.at[half])

    for half in range(halves):
        base = half * tokens
        decay, resid, start = [], [], []
        for m in range(modes):
            at = modes * SUBS + m
            rm = jnp.broadcast_to(state_ref[half, at : at + 1, :], (SUBS, LANES))
            decay.append(jnp.exp(-rm))
            resid.append(jnp.broadcast_to(state_ref[half, at + modes : at + modes + 1, :], (SUBS, LANES)))
            row = half * modes + m
            start.append(
                state_ref[half, m * SUBS : (m + 1) * SUBS, :] + jnp.exp(-rm * runs_left) * enter[row : row + 1]
            )

        def step(i, carry):
            b = steps - 1 - i
            values = step_of(wide_ref, base, b)
            sums = [None] * STEP
            for j in range(STEP - 1, -1, -1):
                carry = tuple(a * w + values[j] for a, w in zip(decay, carry))
                terms = [r * w for r, w in zip(resid, carry)]
                sums[j] = add_up(terms)
            size = STEP * SUBS
            os[pl.ds(pl.multiple_of(b * size, size), size), :] = jnp.concatenate(sums, axis=0)
            return carry

        lax.fori_loop(0, steps, step, tuple(start), unroll=4)

        @pl.loop(0, run // 16, unroll=8)
        def _(i):
            for c in range(SUBS):
                rows = os[pl.ds(i * (16 * SUBS) + c, 16, stride=SUBS), :]
                ob[half, pl.ds(pl.multiple_of(c * run + i * 16, 16), 16), :] = rows.astype(BF16)

        writeback(half).start()
    for half in range(halves):
        writeback(half).wait()


def total_kernel(got_ref, res_ref, lag_ref):
    total = add_up([got_ref[k, :, :] for k in range(got_ref.shape[0])])
    mode = lax.broadcasted_iota(jnp.int32, (SUBS, LANES), 0)
    for j, out in enumerate((res_ref, lag_ref)):
        row = jnp.broadcast_to(total[j : j + 1], (SUBS, LANES))
        tile = row
        for m in range(1, SUBS):
            tile = jnp.where(mode == m, pltpu.roll(row, LANES - OWN * m, 1), tile)
        out[...] = tile[:, :OWN]


def exchange(blocks, axis, order):
    return lax.all_to_all(
        blocks, axis, split_axis=0, concat_axis=0, axis_index_groups=[order], tiled=True
    )


def on_device(grad_out, conv_input, residues, log_rate):
    n_context, n_data = lax.axis_size("ctx"), lax.axis_size("dp")
    tokens, chans = grad_out.shape
    modes = residues.shape[1]
    seqlen = tokens * n_context
    halves = chans // LANES
    params = pltpu.CompilerParams(vmem_limit_bytes=24 * 1024 * 1024)

    send, state, wide, own = pl.pallas_call(
        functools.partial(summary_kernel, float(seqlen)),
        in_specs=[HBM, HBM, HBM, HBM],
        out_specs=[VMEM, VMEM, VMEM, VMEM],
        out_shape=[
            jax.ShapeDtypeStruct((n_context, 3 * SUBS, LANES), BF16),
            jax.ShapeDtypeStruct((halves, modes * SUBS + 2 * modes, LANES), F32),
            jax.ShapeDtypeStruct((halves * tokens, LANES), F32),
            jax.ShapeDtypeStruct((2 * SUBS, LANES), F32),
        ],
        scratch_shapes=[
            pltpu.VMEM((halves, tokens, LANES), BF16),
            pltpu.VMEM((halves, tokens, LANES), BF16),
            pltpu.VMEM((halves, modes, LANES), F32),
            pltpu.VMEM((halves, modes, LANES), F32),
            pltpu.VMEM((tokens, LANES), F32),
            pltpu.VMEM((halves, 6, modes * SUBS, LANES), F32),
            pltpu.SemaphoreType.DMA((8,)),
        ],
        compiler_params=params,
        name="summary",
    )(*(
        pltpu.with_memory_space_constraint(array, pltpu.HBM)
        for array in (grad_out, conv_input, log_rate.T, residues.T)
    ))

    got = exchange(send, "ctx", CTX_ORDER)

    shares = pl.pallas_call(
        functools.partial(join_kernel, float(seqlen), tokens),
        in_specs=[VMEM, VMEM],
        out_specs=VMEM,
        out_shape=jax.ShapeDtypeStruct((n_data, 2, LANES), F32),
        compiler_params=params,
        name="join",
    )(got, own)

    shared = exchange(shares, "dp", DP_ORDER)

    grad_input = pl.pallas_call(
        functools.partial(input_kernel, tokens),
        in_specs=[VMEM, VMEM, VMEM],
        out_specs=HBM,
        out_shape=jax.ShapeDtypeStruct((tokens, chans), BF16),
        scratch_shapes=[
            pltpu.VMEM((tokens, LANES), F32),
            pltpu.VMEM((halves, tokens, LANES), BF16),
            pltpu.SemaphoreType.DMA((2,)),
        ],
        compiler_params=params,
        cost_estimate=pl.CostEstimate(
            flops=4 * tokens * chans * modes, bytes_accessed=4 * tokens * chans, transcendentals=0
        ),
        name="input_gradient",
    )(got, state, wide)

    grad_residue, grad_lograte = pl.pallas_call(
        total_kernel,
        in_specs=[VMEM],
        out_specs=[VMEM, VMEM],
        out_shape=[jax.ShapeDtypeStruct((modes, OWN), F32)] * 2,
        compiler_params=params,
        name="total",
    )(shared)
    return grad_input, grad_residue.T, grad_lograte.T


def solution(mesh):
    in_specs = (P("ctx", "dp"), P("ctx", "dp"), P(), P())
    out_specs = (P("ctx", "dp"), P("ctx", None), P("ctx", None))
    return jax.shard_map(
        on_device, mesh=mesh, in_specs=in_specs, out_specs=out_specs, check_vma=False
    )
```
